512 devices in a mesh: dp: 64 (over x, z), pipe: 8 (over y, core).
Axes of the slice: x: 4, y: 4, z: 16, core: 2. Of those that a mesh axis runs over, the one named last changes fastest.
Arguments:
- grad_partials: bfloat16 [8, 64, 64, 5376], P('pipe', 'dp'), may hold values from -0.796875 to 0.796875
- master: float32 [64, 5376], P('dp'), may hold values from -0.078125 to 0.078125
- moment_one: float32 [64, 5376], P('dp'), may hold values from -2 to 2
- moment_two: float32 [64, 5376], P('dp'), may hold values from 0.01 to 1
- token_rows: int32 [16384], P('dp'), may hold values from 0 to 63
- input_gain: float32 [5376], replicated, may hold values from 0.1 to 1.9
- key_weight: bfloat16 [5376, 1024], P('dp', 'pipe'), may hold values from -0.078125 to 0.078125
- key_gain: float32 [128], replicated, may hold values from 0.1 to 1.9
Outputs:
- new_master: float32 [64, 5376], P('dp')
- new_moment_one: float32 [64, 5376], P('dp')
- new_moment_two: float32 [64, 5376], P('dp')
- section_input: bfloat16 [8, 16384, 5376], P('pipe', 'dp')
- section_keys: bfloat16 [8, 16384, 1024], P('pipe', 'dp')
The draws below stay inside these ranges and needn't reach their ends.
All inputs are finite; a program needn't handle non-finite values.
Results may differ from the reference program's by a relative error of at most 0.0065.
Values may be sent and summed in bfloat16 or wider, within the bound.
A program may use at most 128 MiB of HBM per device.

```python
import math
import jax
import jax.numpy as jnp
from jax import lax

D = 5376
HEAD_DIM = 128
ROWS = 64
TOKENS = 16384
KVW = 1024
N_DP = 64
N_PIPE = 8


def plant(drawn, own_key, least, high):
    dims = drawn.shape
    spot = [jax.random.randint(jax.random.fold_in(own_key, axis), (), 0, dims[axis]) for axis in range(len(dims))]
    drawn = drawn.at[tuple(spot)].set(least)
    longest = dims.index(max(dims))
    spot[longest] = (spot[longest] + 1) % dims[longest]
    return drawn.at[tuple(spot)].set(high)


def spiked(entries, own_key, source, target, blocks, factor):
    owner, partner = [(jnp.arange(entries.shape[axis_at]) // (entries.shape[axis_at] // blocks)).reshape([-1 if axis == axis_at else 1 for axis in range(entries.ndim)]) for axis_at in (source, target)]
    chosen = jax.random.permutation(own_key, blocks)[partner]
    strong = (owner == chosen) | (owner == (partner + blocks // 2) % blocks)
    return jnp.where(strong, factor * entries, entries)


def block_levels(own_key, extent, cuts, low, top_value):
    factor_of, own = 1.0, jax.random.fold_in(own_key, 6)
    for position, blocks in cuts:
        draws = jnp.exp(jax.random.uniform(jax.random.fold_in(own, position), (blocks,), jnp.float32, low / len(cuts), top_value / len(cuts)))
        factor_of = factor_of * jnp.repeat(draws, extent[position] // blocks).reshape([-1 if axis == position else 1 for axis in range(len(extent))])
    return factor_of


def bell_draw(stream_key, dims, scale, reach, split=(), kind=jnp.bfloat16):
    values = jax.random.normal(stream_key, dims, jnp.float32) * scale
    if len(split) > 0:
        values = block_levels(stream_key, dims, split, -0.22, 0.18) * values
    return jnp.clip(values, min=-reach, max=reach).astype(kind)


def gaussian_with(rng, shape, spread, limit, pieces, heavy, kind=jnp.bfloat16):
    values = spread * jax.random.normal(rng, shape, jnp.float32)
    if pieces:
        values = values * block_levels(rng, shape, pieces, -0.22, 0.18)
    return jnp.clip(spiked(values, jax.random.fold_in(rng, 3), *heavy), -limit, limit).astype(kind)


def setup_inputs(seed: int = 0) -> dict:
    key_list = jax.random.split(jax.random.key(seed), 9)
    return {
        "grad_partials": gaussian_with(key_list[0], (N_PIPE, N_DP, ROWS, D), 0.1, 0.796875, ((0, 8), (1, 64)), (1, 2, 64, 4.0)),
        "master": bell_draw(key_list[1], (ROWS, D), D ** -0.5, 0.078125, ((0, 64),), jnp.float32),
        "moment_one": bell_draw(key_list[2], (ROWS, D), 0.3, 2.0, ((0, 64),), jnp.float32),
        "moment_two": jnp.clip(jnp.exp(math.log(1.0) - 4.6051702 * jax.random.uniform(key_list[3], (ROWS, D), jnp.float32) ** block_levels(key_list[3], (ROWS, D), ((0, 64),), -0.2, 0.2)), 0.01, 1.0),
        "token_rows": plant(jax.random.randint(key_list[4], (TOKENS,), 0, ROWS), jax.random.fold_in(key_list[4], 1), 0, ROWS - 1).astype(jnp.int32),
        "input_gain": jnp.clip(1.0 + 0.18 * jax.random.normal(key_list[5], (D,), jnp.float32), 0.1, 1.9),
        "key_weight": bell_draw(key_list[6], (D, KVW), D ** -0.5, 0.078125, ((0, 64), (1, 8))),
        "key_gain": jnp.clip(1.0 + 0.18 * jax.random.normal(key_list[7], (HEAD_DIM,), jnp.float32), 0.1, 1.9),
    }


def head_norm(raw_keys, key_gain):
    blocks = raw_keys.reshape(raw_keys.shape[0], -1, HEAD_DIM)
    scaled = blocks * lax.rsqrt(lax.optimization_barrier(jnp.mean(blocks * blocks, axis=-1, keepdims=True)) + 1e-06) * key_gain
    return scaled.reshape(raw_keys.shape).astype(jnp.bfloat16)

def reference(grad_partials, master, moment_one, moment_two, token_rows, input_gain, key_weight, key_gain):
    grad_first = grad_partials[0].astype(jnp.float32)
    grad_last = grad_partials[N_PIPE - 1].astype(jnp.float32)
    gradient = lax.optimization_barrier(jnp.sum(grad_first, axis=0)) + lax.optimization_barrier(jnp.sum(grad_last, axis=0))
    new_moment_one = 0.9 * moment_one + 0.1 * gradient
    new_moment_two = 0.95 * moment_two + 0.05 * gradient * gradient
    correct_one = 1.0 - 0.9 ** 10
    correct_two = 1.0 - 0.95 ** 10
    update = new_moment_one / correct_one / (jnp.sqrt(new_moment_two / correct_two) + 1e-08)
    new_master = master - 0.001 * update
    table = new_master.astype(jnp.bfloat16)
    one_hot = (token_rows[:, None] == jnp.arange(ROWS, dtype=jnp.int32)[None, :]).astype(jnp.bfloat16)
    looked = jnp.dot(one_hot, table, preferred_element_type=jnp.float32)
    embedded = (looked * jnp.float32(D ** 0.5)).astype(jnp.bfloat16)
    wide = embedded.astype(jnp.float32)
    normed = (wide * lax.rsqrt(lax.optimization_barrier(jnp.mean(wide * wide, axis=-1, keepdims=True)) + 1e-06) * input_gain).astype(jnp.bfloat16)
    raw_keys = jnp.dot(normed, key_weight, preferred_element_type=jnp.float32)
    keys = head_norm(raw_keys, key_gain)
    receiving = jnp.arange(N_PIPE, dtype=jnp.int32) == 1 % N_PIPE
    zero_value = jnp.zeros((), jnp.bfloat16)
    section_input = jnp.where(receiving[:, None, None], embedded[None], zero_value)
    section_keys = jnp.where(receiving[:, None, None], keys[None], zero_value)
    return (new_master, new_moment_one, new_moment_two, section_input, section_keys)
```

```python
import jax
import jax.numpy as jnp
from jax import lax
from jax.experimental import pallas as pl
from jax.experimental.pallas import tpu as pltpu
from jax.sharding import PartitionSpec as P

MESH = pl.DeviceIdType.MESH
HEAD_DIM = 128
LANES = 128
NX, NZ, NP = 4, 16, 8
D = 5376
NCH = D // LANES
PAD = 48
WROWS = 84
WPAD = 96
KC = 11
KW = KC * LANES
HEADS2 = 2 * HEAD_DIM

(
    XS, XR, XL, ZS, ZR, YS, YR0, YR1, W0S, W0R, WAS, WAR, WBS, WB1, WB2, WB3,
    ES, ER, KS, KR, FS, FR, PS, PR, OUT,
) = range(25)


def first_chunk(x):
    return (x // 2) * 21 + lax.rem(x, 2) * 10


def comm_kernel(
    grad, master, moment_one, moment_two, weight, gain,
    table_out, keys_out, master_out, one_out, two_out,
    gx, zs, zb, zr, yr, prior, erow, ezr, ef, block, full, part, wc, wp, wz, wf, wk, kp, sem,
):
    dp = lax.axis_index("dp")
    pipe = lax.axis_index("pipe")
    x, z = dp // NZ, lax.rem(dp, NZ)
    y, core = pipe // 2, lax.rem(pipe, 2)
    holder = jnp.logical_or(pipe == 0, pipe == NP - 1)
    ringer = jnp.logical_or(holder, core == 1)
    last = pipe == NP - 1
    lead = pipe == 1
    odd = core == 1

    def at(x_to, z_to, pipe_to):
        return (x_to * NZ + z_to, pipe_to)

    def send(src, dst, sent, arrived, where):
        pltpu.make_async_remote_copy(
            src_ref=src, dst_ref=dst, send_sem=sem.at[sent], recv_sem=sem.at[arrived],
            device_id=where, device_id_type=MESH,
        ).start()

    def wait_for(like, which):
        pltpu.make_async_copy(like, like, sem.at[which]).wait()

    barrier = pltpu.get_barrier_semaphore()

    def tell(where):
        pl.semaphore_signal(barrier, inc=1, device_id=where, device_id_type=MESH)

    @pl.when(ringer)
    def _():
        @pl.loop(1, NZ)
        def _(k):
            tell(at(x, lax.rem(z + k, NZ), pipe))

        for k in range(1, NX):
            tell(at(lax.rem(x + k, NX), z, pipe))

    @pl.when(pipe != 0)
    def _():
        tell((dp, 0))

    @pl.when(jnp.logical_not(last))
    def _():
        tell((dp, NP - 1))

    @pl.when(jnp.logical_and(odd, jnp.logical_not(lead)))
    def _():
        tell((dp, pipe - 1))

    @pl.when(lead)
    def _():
        for k in range(NX):
            for q in range(3, NP, 2):
                if k > 0 or q < NP - 1:
                    tell(at(lax.rem(x + k, NX), z, q))

    wc[...] = jnp.zeros_like(wc)
    wc[0:WROWS, :] = weight[...]

    peers = NZ - 1 + NX - 1
    for q in range(NP):
        count = (peers if q in (0, NP - 1) or q % 2 else 0) + (NP - 1 if q in (0, NP - 1) else 0)
        count += 1 if q % 2 == 0 and q != 0 else 0
        count += NX if q % 2 and q not in (1, NP - 1) else 0
        count += NX - 1 if q == NP - 1 else 0

        @pl.when(pipe == q)
        def _(count=count):
            pl.semaphore_wait(barrier, count)

    @pl.when(holder)
    def _():
        for k in range(1, NX):
            to = lax.rem(x + k, NX)
            rows = pl.ds(pl.multiple_of(to * NZ, NZ), NZ)
            send(grad.at[0, 0, rows, :], gx.at[x], XS, XR, at(to, z, pipe))
        rows = pl.ds(pl.multiple_of(x * NZ, NZ), NZ)
        pltpu.make_async_copy(grad.at[0, 0, rows, :], gx.at[x], sem.at[XL]).start()

    @pl.when(jnp.logical_not(odd))
    def _():
        send(wc, wp.at[:, 0:LANES], W0S, W0R, (dp, pipe + 1))

    mine = lax.rem(z, 4)

    @pl.when(odd)
    def _():
        wp[:, LANES:HEADS2] = wc[...]
        wait_for(wc, W0R)
        for k in range(1, 4):
            send(wp, wz.at[mine, z // 4], WAS, WAR, at(x, lax.rem(z + 4 * k, NZ), pipe))
        wz[mine, z // 4] = wp[...]

    def weights_on():
        wait_for(wz.at[0, 0:3], WAR)
        send(wz.at[mine], wz.at[mine], WBS, WB1, at(x, lax.rem(z + 1, NZ), pipe))
        send(wz.at[mine], wz.at[mine], WBS, WB2, at(x, lax.rem(z + NZ - 1, NZ), pipe))
        two = z + 2 + lax.rem(z, 2) * (NZ - 4)
        send(wz.at[mine], wz.at[mine], WBS, WB3, at(x, lax.rem(two, NZ), pipe))

    @pl.when(jnp.logical_and(odd, jnp.logical_not(last)))
    def _():
        weights_on()

    prior[...] = jnp.zeros_like(prior)

    @pl.loop(0, NCH)
    def _(j):
        lanes = pl.ds(pl.multiple_of(j * LANES, LANES), LANES)
        prior[0, pl.ds(j, 1), :] = master[:, lanes]
        prior[1, pl.ds(j, 1), :] = moment_one[:, lanes]
        prior[2, pl.ds(j, 1), :] = moment_two[:, lanes]

    @pl.when(holder)
    def _():
        zs[...] = jnp.zeros_like(zs)
        wait_for(gx.at[0], XL)
        wait_for(gx.at[0:3], XR)

        @pl.loop(0, NCH)
        def _(j):
            lanes = pl.ds(pl.multiple_of(j * LANES, LANES), LANES)
            total = gx[0, :, lanes].astype(jnp.float32)
            for k in range(1, NX):
                total = total + gx[k, :, lanes].astype(jnp.float32)
            zs[pl.ds(j, NZ, stride=PAD), :] = total

        zb[...] = zs[...].reshape(NZ, PAD, LANES).astype(jnp.bfloat16)

        @pl.loop(1, NZ)
        def _(k):
            to = lax.rem(z + k, NZ)
            send(zb.at[to], zr.at[z], ZS, ZR, at(x, to, pipe))

        zr[z] = zb[z]

    @pl.when(last)
    def _():
        weights_on()

    @pl.when(holder)
    def _():
        wait_for(zr.at[0 : NZ - 1], ZR)
        total = zr[0].astype(jnp.float32)
        for k in range(1, NZ):
            total = total + zr[k].astype(jnp.float32)

        @pl.when(pipe == 0)
        def _():
            yr[0] = total
            for q in range(1, NP):
                send(yr.at[0], yr.at[0], YS, YR0, (dp, q))

        @pl.when(last)
        def _():
            yr[1] = total
            for q in range(NP - 1):
                send(yr.at[1], yr.at[1], YS, YR1, (dp, q))

    @pl.when(pipe != 0)
    def _():
        wait_for(yr.at[0], YR0)

    @pl.when(jnp.logical_not(last))
    def _():
        wait_for(yr.at[1], YR1)

    gradient = yr[0] + yr[1]
    new_one = 0.9 * prior[1] + 0.1 * gradient
    new_two = 0.95 * prior[2] + 0.05 * gradient * gradient
    correct_one = 1.0 - 0.9**10
    correct_two = 1.0 - 0.95**10
    update = new_one / correct_one / (jnp.sqrt(new_two / correct_two) + 1e-08)
    new_master = prior[0] - 0.001 * update

    @pl.when(odd)
    def _():
        table = new_master.astype(jnp.bfloat16).astype(jnp.float32)
        erow[...] = (table * jnp.float32(D**0.5)).astype(jnp.bfloat16)

        @pl.loop(1, NZ)
        def _(k):
            send(erow, ezr.at[z], ES, ER, at(x, lax.rem(z + k, NZ), pipe))

        ezr[z] = erow[...]

    master_out[...] = new_master
    one_out[...] = new_one
    two_out[...] = new_two

    @pl.when(odd)
    def _():
        wait_for(wz.at[0], WB1)
        wait_for(wz.at[0], WB2)
        wait_for(wz.at[0], WB3)
        side = lax.rem(x, 2)
        spare = pl.multiple_of((1 - side) * NZ * WROWS, 64)
        wk[pl.ds(spare, 64), :] = jnp.zeros((64, HEADS2), jnp.bfloat16)

        @pl.loop(0, 4)
        def _(g):
            for k in range(4):
                wf[WROWS * k : WROWS * (k + 1), :] = wz[k, g, 0:WROWS, :].astype(jnp.float32)
            start = pl.multiple_of(side * 64 + g * 4 * WROWS, 16)
            wk[pl.ds(start, 4 * WROWS), :] = wf[...].astype(jnp.bfloat16)

        wait_for(ezr.at[0 : NZ - 1], ER)
        ef[...] = ezr[...].astype(jnp.float32).reshape(NZ * PAD, LANES)

        @pl.loop(0, NCH)
        def _(j):
            lanes = pl.ds(pl.multiple_of(j * LANES, LANES), LANES)
            block[:, lanes] = ef[pl.ds(j, NZ, stride=PAD), :].astype(jnp.bfloat16)

        def features(x_of):
            return pl.ds(pl.multiple_of(first_chunk(x_of) * LANES, LANES), KW)

        for k in range(1, NX):
            to = lax.rem(x + k, NX)
            send(block.at[:, features(to)], part.at[x], KS, KR, at(to, z, pipe))

        @pl.when(lead)
        def _():
            for k in range(1, NX):
                send(block, full.at[x], FS, FR, at(lax.rem(x + k, NX), z, pipe))
            full[x] = block[...]

        part[x] = block[:, features(x)]
        wait_for(part.at[0:3], KR)
        scaled = part[...].reshape(NX * NZ, KW).astype(jnp.float32) * gain[:, features(x)]
        product = jnp.dot(
            scaled.astype(jnp.bfloat16), wk[...], preferred_element_type=jnp.float32
        )
        slot = y * NX + x
        kp[slot] = product.astype(jnp.bfloat16)
        for k in range(NX):
            to = lax.rem(x + k, NX)

            def share(to=to):
                send(kp.at[slot], kp.at[slot], PS, PR, at(to, z, 1))

            if k:
                share()
            else:
                pl.when(jnp.logical_not(lead))(share)

    @pl.when(lead)
    def _():
        wait_for(full.at[0:3], FR)
        out = pltpu.make_async_copy(full, table_out, sem.at[OUT])
        out.start()
        squares = jnp.zeros((NX * NZ, LANES), jnp.float32)
        for j in range(NCH):
            wide = full[:, :, LANES * j : LANES * (j + 1)].astype(jnp.float32)
            wide = wide.reshape(NX * NZ, LANES)
            squares = squares + wide * wide
        scale = lax.rsqrt(jnp.sum(squares, axis=-1, keepdims=True) / D + 1e-06)
        wait_for(kp.at[0 : NX * NP // 2 - 1], PR)
        for s in range(NP // 2):
            raw = kp[s * NX].astype(jnp.float32)
            for k in range(1, NX):
                raw = raw + kp[s * NX + k].astype(jnp.float32)
            raw = raw * scale
            for h in range(2):
                head = raw[:, h * HEAD_DIM : (h + 1) * HEAD_DIM]
                keys_out[:, s * HEADS2 + h * HEAD_DIM : s * HEADS2 + (h + 1) * HEAD_DIM] = (
                    head * lax.rsqrt(jnp.mean(head * head, axis=-1, keepdims=True) + 1e-06)
                )
        out.wait()

    @pl.when(holder)
    def _():
        wait_for(gx.at[0:3], XS)
        wait_for(zr.at[0 : NZ - 1], ZS)
        for q in range(NP - 1):
            wait_for(yr.at[0], YS)

    @pl.when(jnp.logical_not(odd))
    def _():
        wait_for(wc, W0S)

    @pl.when(odd)
    def _():
        wait_for(wz.at[0, 0:3], WAS)
        wait_for(wz.at[0:3], WBS)
        wait_for(ezr.at[0 : NZ - 1], ES)
        wait_for(part.at[0:3], KS)
        wait_for(kp.at[0:3], PS)

        @pl.when(lead)
        def _():
            wait_for(full.at[0:3], FS)

        @pl.when(jnp.logical_not(lead))
        def _():
            wait_for(kp.at[0], PS)


TOKEN_BLOCK = 64


def lookup_kernel(
    table, keys, key_gain, tokens, master, one, two,
    master_out, one_out, two_out, section_input, section_keys,
):
    lead = lax.axis_index("pipe") == 1

    @pl.when(pl.program_id(0) == 0)
    def _():
        @pl.loop(0, NCH)
        def _(j):
            lanes = pl.ds(pl.multiple_of(j * LANES, LANES), LANES)
            master_out[:, lanes] = master[pl.ds(j, 1), :]
            one_out[:, lanes] = one[pl.ds(j, 1), :]
            two_out[:, lanes] = two[pl.ds(j, 1), :]

    @pl.when(lead)
    def _():
        rows = table.shape[0]
        count = section_input.shape[1]
        start = pl.multiple_of(pl.program_id(0) * count, count)
        hot = lax.broadcasted_iota(jnp.int32, (count, rows), 1) == tokens[pl.ds(start, count), :]
        hot = hot.astype(jnp.bfloat16)
        section_input[0] = jnp.dot(
            hot, table[...], preferred_element_type=jnp.float32
        ).astype(jnp.bfloat16)
        gains = jnp.concatenate([key_gain[...]] * (keys.shape[1] // HEAD_DIM), axis=1)
        rounded = (keys[...] * gains).astype(jnp.bfloat16)
        section_keys[0] = jnp.dot(
            hot, rounded, preferred_element_type=jnp.float32
        ).astype(jnp.bfloat16)

    @pl.when(jnp.logical_not(lead))
    def _():
        section_input[...] = jnp.zeros_like(section_input)
        section_keys[...] = jnp.zeros_like(section_keys)


def shards(
    grad_partials, master, moment_one, moment_two, token_rows, input_gain, key_weight, key_gain
):
    rows, kvw = NX * NZ, NP * HEAD_DIM
    bf16, f32 = jnp.bfloat16, jnp.float32
    vmem = pl.BlockSpec(memory_space=pltpu.VMEM)
    hbm = pl.BlockSpec(memory_space=pl.ANY)
    line = jax.ShapeDtypeStruct((PAD, LANES), f32)
    table, keys, row, row_one, row_two = pl.pallas_call(
        comm_kernel,
        out_shape=(
            jax.ShapeDtypeStruct((NX, NZ, D), bf16),
            jax.ShapeDtypeStruct((rows, kvw), f32),
            line, line, line,
        ),
        in_specs=[hbm, vmem, vmem, vmem, vmem, vmem],
        out_specs=(hbm, vmem, vmem, vmem, vmem),
        scratch_shapes=[
            pltpu.VMEM((NX, NZ, D), bf16),
            pltpu.VMEM((NZ * PAD, LANES), f32),
            pltpu.VMEM((NZ, PAD, LANES), bf16),
            pltpu.VMEM((NZ, PAD, LANES), bf16),
            pltpu.VMEM((2, PAD, LANES), f32),
            pltpu.VMEM((3, PAD, LANES), f32),
            pltpu.VMEM((PAD, LANES), bf16),
            pltpu.VMEM((NZ, PAD, LANES), bf16),
            pltpu.VMEM((NZ * PAD, LANES), f32),
            pltpu.VMEM((NZ, D), bf16),
            pltpu.VMEM((NX, NZ, D), bf16),
            pltpu.VMEM((NX, NZ, KW), bf16),
            pltpu.VMEM((WPAD, LANES), bf16),
            pltpu.VMEM((WPAD, HEADS2), bf16),
            pltpu.VMEM((4, 4, WPAD, HEADS2), bf16),
            pltpu.VMEM((4 * WROWS, HEADS2), f32),
            pltpu.VMEM((KW, HEADS2), bf16),
            pltpu.VMEM((NX * NP // 2, rows, HEADS2), bf16),
            pltpu.SemaphoreType.DMA((25,)),
        ],
        compiler_params=pltpu.CompilerParams(
            collective_id=0, has_side_effects=True, vmem_limit_bytes=32 * 2**20
        ),
        name="sum_step_gather",
    )(grad_partials, master, moment_one, moment_two, key_weight, input_gain.reshape(1, D))

    count = token_rows.shape[0]
    whole = pl.BlockSpec((1, D), lambda i: (0, 0))
    new_master, new_one, new_two, section_input, section_keys = pl.pallas_call(
        lookup_kernel,
        grid=(count // TOKEN_BLOCK,),
        out_shape=(
            jax.ShapeDtypeStruct((1, D), f32),
            jax.ShapeDtypeStruct((1, D), f32),
            jax.ShapeDtypeStruct((1, D), f32),
            jax.ShapeDtypeStruct((1, count, D), bf16),
            jax.ShapeDtypeStruct((1, count, kvw), bf16),
        ),
        in_specs=[vmem] * 7,
        out_specs=(
            whole, whole, whole,
            pl.BlockSpec((1, TOKEN_BLOCK, D), lambda i: (0, i, 0)),
            pl.BlockSpec((1, TOKEN_BLOCK, kvw), lambda i: (0, i, 0)),
        ),
        compiler_params=pltpu.CompilerParams(vmem_limit_bytes=32 * 2**20),
        name="look_up",
    )(
        table.reshape(rows, D), keys, key_gain.reshape(1, HEAD_DIM), token_rows.reshape(count, 1),
        row, row_one, row_two,
    )
    return new_master, new_one, new_two, section_input, section_keys


def solution(mesh):
    in_specs = (
        P("pipe", "dp", None, None),
        P("dp", None),
        P("dp", None),
        P("dp", None),
        P("dp"),
        P(),
        P("dp", "pipe"),
        P(),
    )
    out_specs = (
        P("dp", None),
        P("dp", None),
        P("dp", None),
        P("pipe", "dp", None),
        P("pipe", "dp", None),
    )
    return jax.shard_map(shards, mesh=mesh, in_specs=in_specs, out_specs=out_specs, check_vma=False)
```

```python
import jax
import jax.numpy as jnp
from jax import lax
from jax.experimental import pallas as pl
from jax.experimental.pallas import tpu as pltpu
from jax.sharding import PartitionSpec as P

MESH = pl.DeviceIdType.MESH
HEAD_DIM = 128
LANES = 128
NX, NZ, NP = 4, 16, 8
D = 5376
NCH = D // LANES
PAD = 48
WROWS = 84
WPAD = 96
KC = 11
KW = KC * LANES
HEADS2 = 2 * HEAD_DIM
VMEM_BYTES = 60 * 2**20

(
    XS, XR, ZS, ZR, RP, RM, YS, YR0, YR1, W0S, W0R, WAS, WM, WP, W8, WBS, WB0, WB1, WB2, WB3,
    ES, EM, EP, ER, KS, KR, FS, FR, PS, PR, LM, L1, L2, LW, LG, LK, O1, O2, O3,
) = range(39)
REACH = 4


def first_chunk(x):
    return (x // 2) * 21 + lax.rem(x, 2) * 10


def comm_kernel(
    grad, master, moment_one, moment_two, weight, gain, key_gain,
    table_out, keys_out, step_out,
    gx, zs, zb, zr, zp, zm, zq, yr, state, prior, erow, ezr, ef, block, full, part, wv, wc, wp, wg, wz, wf, wk, kp,
    gv, gl, kg, step, keys, sem,
):
    dp = lax.axis_index("dp")
    pipe = lax.axis_index("pipe")
    x, z = dp // NZ, lax.rem(dp, NZ)
    y = pipe // 2
    far = y == NP // 2 - 1
    worker = jnp.where(far, 2 * y, 2 * y + 1) == pipe
    mate = jnp.where(lax.rem(pipe, 2) == 0, pipe + 1, pipe - 1)
    source = jnp.logical_or(pipe == 0, pipe == NP - 1)
    lead, last = pipe == 1, pipe == NP - 2
    reducer = jnp.logical_or(lead, last)

    def at(x_to, z_to, pipe_to):
        return (x_to * NZ + z_to, pipe_to)

    def send(src, dst, sent, arrived, where):
        pltpu.make_async_remote_copy(
            src_ref=src, dst_ref=dst, send_sem=sem.at[sent], recv_sem=sem.at[arrived],
            device_id=where, device_id_type=MESH,
        ).start()

    def wait_for(like, which):
        pltpu.make_async_copy(like, like, sem.at[which]).wait()

    barrier = pltpu.get_barrier_semaphore()

    def tell(where):
        pl.semaphore_signal(barrier, inc=1, device_id=where, device_id_type=MESH)

    def away(k):
        return lax.rem(z + k + NZ, NZ)

    near = [k for k in range(-REACH, REACH + 1) if k]

    two = 2 - 4 * lax.rem(z, 2)

    @pl.when(worker)
    def _():
        for k in near:
            tell(at(x, away(k), pipe))
        for k in range(1, NX):
            tell(at(lax.rem(x + k, NX), z, pipe))
        for k in (0, 1, -1, -two):
            tell(at(x, away(k), mate))

    @pl.when(reducer)
    def _():
        for k in range(1, NX):
            tell(at(lax.rem(x + k, NX), z, mate))

    @pl.when(jnp.logical_not(worker))
    def _():
        tell(at(x, away(REACH), pipe))
        tell(at(x, away(-REACH), pipe))

    @pl.when(jnp.logical_or(pipe == 2, pipe == 4))
    def _():
        tell((dp, mate))

    @pl.when(jnp.logical_not(lead))
    def _():
        tell((dp, 1))

    @pl.when(jnp.logical_not(last))
    def _():
        tell((dp, NP - 2))

    @pl.when(lead)
    def _():
        for k in range(NX):
            for q in (3, 5, 6):
                if k > 0 or q != 6:
                    tell(at(lax.rem(x + k, NX), z, q))

    def load(src, dst, which):
        copy = pltpu.make_async_copy(src, dst, sem.at[which])
        copy.start()
        return copy

    load_weight = load(weight, wv, LW)
    load_state = [
        load(master, state.at[0], LM), load(moment_one, state.at[1], L1),
        load(moment_two, state.at[2], L2),
    ]
    load_gain = load(gain, gv, LG)
    load_key_gain = load(key_gain, kg, LK)

    peers = len(near) + NX - 1
    counts = {
        0: 6 + NX - 1, NP - 1: 6 + NX - 1, 2: 6, 4: 6,
        1: peers + NP - 1, 6: peers + NP - 1 + NX - 1, 3: peers + NX + 1, 5: peers + NX + 1,
    }
    for q, count in counts.items():

        @pl.when(pipe == q)
        def _(count=count):
            pl.semaphore_wait(barrier, count)

    @pl.when(source)
    def _():
        for k in range(NX):
            to = lax.rem(x + k, NX)
            rows = pl.ds(pl.multiple_of(to * NZ, NZ), NZ)
            send(grad.at[0, 0, rows, :], gx.at[x], XS, XR, at(to, z, mate))

    load_weight.wait()
    wc[...] = jnp.zeros_like(wc)
    wide = wv[...].astype(jnp.float32)
    for q in range(4):
        @pl.when(lax.rem(z, 4) == q)
        def _(q=q):
            wf[...] = jnp.zeros_like(wf)
            wf[4 * q : 4 * q + WROWS, :] = wide
            wc[...] = wf[...].astype(jnp.bfloat16)

    for high in (False, True):
        lanes = slice(LANES, HEADS2) if high else slice(0, LANES)

        @pl.when((lax.rem(pipe, 2) == 1) == high)
        def _(lanes=lanes):
            @pl.when(worker)
            def _():
                send(wc, wp.at[:, lanes], W0S, W0R, (dp, mate))

            @pl.when(jnp.logical_not(worker))
            def _():
                wp[:, lanes] = wc[...]

    @pl.when(jnp.logical_not(worker))
    def _():
        mine = lax.rem(z, 4)
        wait_for(wc, W0R)
        send(wp, wg.at[z // 4], WAS, WM, at(x, away(REACH), pipe))
        send(wp, wg.at[z // 4], WAS, WP, at(x, away(-REACH), pipe))
        wg[z // 4] = wp[...]
        wait_for(wp, WM)
        back = lax.rem(z // 4 + 3, 4)
        send(wg.at[back], wg.at[back], WAS, W8, at(x, away(REACH), pipe))
        wait_for(wp, WP)
        wait_for(wp, W8)
        for k, which in ((two, WB3), (1, WB1), (-1, WB2), (0, WB0)):
            send(wg, wz.at[mine], WBS, which, at(x, away(k), mate))

    prior[...] = jnp.zeros_like(prior)
    for copy in load_state:
        copy.wait()
    for j in range(NCH):
        lanes = slice(j * LANES, (j + 1) * LANES)
        prior[0, j : j + 1, :] = state[0, :, lanes]
        prior[1, j : j + 1, :] = state[1, :, lanes]
        prior[2, j : j + 1, :] = state[2, :, lanes]

    load_gain.wait()
    load_key_gain.wait()

    def weights_join():
        wait_for(wz.at[0], WB0)
        wait_for(wz.at[0], WB1)
        wait_for(wz.at[0], WB2)
        wait_for(wz.at[0], WB3)
        side = lax.rem(x, 2)
        spare = pl.multiple_of((1 - side) * NZ * WROWS, 64)
        wk[pl.ds(spare, 64), :] = jnp.zeros((64, HEADS2), jnp.bfloat16)
        for g in range(4):
            start = pl.multiple_of(side * 64 + g * 4 * WROWS, 16)

            def put(row, value):
                wk[pl.ds(pl.multiple_of(start + row, 16), value.shape[0]), :] = value

            for k in range(4):
                edge = wz[k, g, 0:16, :]
                if k:
                    edge = edge + wz[k - 1, g, 80:96, :]
                put(80 * k, edge)
                put(80 * k + 16, wz[k, g, 16:80, :])
            put(320, wz[3, g, 80:96, :])
        for j in range(NCH):
            gl[:, j * LANES : (j + 1) * LANES] = gv[j : j + 1, :]

    def row_sum(refs):
        total = refs[0].astype(jnp.float32)
        for ref in refs[1:]:
            total = total + ref.astype(jnp.float32)
        return total

    @pl.when(reducer)
    def _():
        zs[...] = jnp.zeros_like(zs)
        wait_for(gx, XR)
        for j in range(NCH):
            lanes = slice(j * LANES, (j + 1) * LANES)
            total = row_sum([gx[k, :, lanes] for k in range(NX)])
            zs[pl.ds(j, NZ, stride=PAD), :] = total
        zb[...] = zs[...].reshape(NZ, PAD, LANES).astype(jnp.bfloat16)

        for k in range(REACH, 0, -1):
            send(zb.at[away(k + REACH)], zp.at[k - 1], ZS, RP, at(x, away(k), pipe))
            if k < REACH:
                send(zb.at[away(-k - REACH)], zm.at[k - 1], ZS, RM, at(x, away(-k), pipe))
        for k in range(1, REACH):
            send(zb.at[away(k)], zr.at[REACH - k], ZS, ZR, at(x, away(k), pipe))
            send(zb.at[away(-k)], zr.at[REACH + k - 1], ZS, ZR, at(x, away(-k), pipe))

        def pass_up():
            wait_for(zp, RP)
            own = zs[pl.ds(pl.multiple_of(away(REACH) * PAD, PAD), PAD), :]
            zq[0] = (own + row_sum([zp[k] for k in range(REACH)])).astype(jnp.bfloat16)
            send(zq.at[0], zr.at[0], ZS, ZR, at(x, away(REACH), pipe))

        def pass_down():
            wait_for(zm, RM)
            own = zs[pl.ds(pl.multiple_of(away(-REACH) * PAD, PAD), PAD), :]
            zq[1] = (own + row_sum([zm[k] for k in range(REACH - 1)])).astype(jnp.bfloat16)
            send(zq.at[1], zr.at[2 * REACH - 1], ZS, ZR, at(x, away(-REACH), pipe))

        @pl.when(z < NZ // 2)
        def _():
            pass_up()
            pass_down()

        @pl.when(z >= NZ // 2)
        def _():
            pass_down()
            pass_up()

    @pl.when(reducer)
    def _():
        wait_for(zr, ZR)
        own = zs[pl.ds(pl.multiple_of(z * PAD, PAD), PAD), :]
        total = own + row_sum([zr[k] for k in range(2 * REACH)])

        @pl.when(lead)
        def _():
            yr[0] = total
            for q in (3, 5, 6, 0, 2, 4, 7):
                send(yr.at[0], yr.at[0], YS, YR0, (dp, q))

        @pl.when(last)
        def _():
            yr[1] = total
            for q in (1, 3, 5, 0, 2, 4, 7):
                send(yr.at[1], yr.at[1], YS, YR1, (dp, q))

    @pl.when(jnp.logical_not(lead))
    def _():
        wait_for(yr.at[0], YR0)

    @pl.when(jnp.logical_not(last))
    def _():
        wait_for(yr.at[1], YR1)

    gradient = yr[0] + yr[1]
    new_one = 0.9 * prior[1] + 0.1 * gradient
    new_two = 0.95 * prior[2] + 0.05 * gradient * gradient
    correct_one = 1.0 - 0.9**10
    correct_two = 1.0 - 0.95**10
    update = new_one / correct_one / (jnp.sqrt(new_two / correct_two) + 1e-08)
    new_master = prior[0] - 0.001 * update
    step[0] = new_master
    step[1] = new_one
    step[2] = new_two
    keep = pltpu.make_async_copy(step, step_out, sem.at[O1])

    @pl.when(worker)
    def _():
        table = new_master.astype(jnp.bfloat16).astype(jnp.float32)
        erow[...] = (table * jnp.float32(D**0.5)).astype(jnp.bfloat16)
        for k in (4, -4, 3, -3, 2, -2, 1, -1):
            arrives = {REACH: EM, -REACH: EP}.get(k, ER)
            send(erow, ezr.at[z], ES, arrives, at(x, away(k), pipe))
        ezr[z] = erow[...]

    keep.start()

    @pl.when(worker)
    def _():
        def pass_up():
            wait_for(erow, EM)
            row = away(-REACH)
            for k in range(REACH, 0, -1):
                send(ezr.at[row], ezr.at[row], ES, ER, at(x, away(k), pipe))

        def pass_down():
            wait_for(erow, EP)
            row = away(REACH)
            for k in range(REACH - 1, 0, -1):
                send(ezr.at[row], ezr.at[row], ES, ER, at(x, away(-k), pipe))

        @pl.when(z < NZ // 2)
        def _():
            pass_down()
            pass_up()

        @pl.when(z >= NZ // 2)
        def _():
            pass_up()
            pass_down()

        weights_join()

        wait_for(ezr.at[0 : NZ - 3], ER)
        ef[...] = ezr[...].astype(jnp.float32).reshape(NZ * PAD, LANES)

        for j in range(NCH):
            lanes = slice(j * LANES, (j + 1) * LANES)
            block[:, lanes] = ef[pl.ds(j, NZ, stride=PAD), :].astype(jnp.bfloat16)

        def features(x_of):
            return pl.ds(pl.multiple_of(first_chunk(x_of) * LANES, LANES), KW)

        for k in range(1, NX):
            to = lax.rem(x + k, NX)
            send(block.at[:, features(to)], part.at[x], KS, KR, at(to, z, pipe))

        @pl.when(lead)
        def _():
            for k in range(1, NX):
                send(block, full.at[x], FS, FR, at(lax.rem(x + k, NX), z, pipe))
            full[x] = block[...]

        part[x] = block[:, features(x)]
        wait_for(part.at[0:3], KR)
        scaled = part[...].reshape(NX * NZ, KW).astype(jnp.float32) * gl[:, features(x)]
        product = jnp.dot(
            scaled.astype(jnp.bfloat16), wk[...], preferred_element_type=jnp.float32
        )
        slot = y * NX + x
        kp[slot] = product.astype(jnp.bfloat16)
        for k in range(NX):
            to = lax.rem(x + k, NX)

            def share(to=to):
                send(kp.at[slot], kp.at[slot], PS, PR, at(to, z, 1))

            if k:
                share()
            else:
                pl.when(jnp.logical_not(lead))(share)

    @pl.when(lead)
    def _():
        wait_for(full.at[0:3], FR)
        out = pltpu.make_async_copy(full, table_out, sem.at[O2])
        out.start()
        squares = jnp.zeros((NX * NZ, LANES), jnp.float32)
        for j in range(NCH):
            wide = full[:, :, LANES * j : LANES * (j + 1)].astype(jnp.float32)
            wide = wide.reshape(NX * NZ, LANES)
            squares = squares + wide * wide
        scale = lax.rsqrt(jnp.sum(squares, axis=-1, keepdims=True) / D + 1e-06)
        wait_for(kp.at[0 : NX * NP // 2 - 1], PR)
        for s in range(NP // 2):
            raw = kp[s * NX].astype(jnp.float32)
            for k in range(1, NX):
                raw = raw + kp[s * NX + k].astype(jnp.float32)
            raw = raw * scale
            for h in range(2):
                head = raw[:, h * HEAD_DIM : (h + 1) * HEAD_DIM]
                mean = jnp.mean(head * head, axis=-1, keepdims=True)
                first = s * HEADS2 + h * HEAD_DIM
                keys[:, first : first + HEAD_DIM] = (
                    head * lax.rsqrt(mean + 1e-06) * kg[...]
                ).astype(jnp.bfloat16)
        last_out = pltpu.make_async_copy(keys, keys_out, sem.at[O3])
        last_out.start()
        out.wait()
        last_out.wait()

    keep.wait()

    @pl.when(source)
    def _():
        wait_for(gx, XS)

    @pl.when(reducer)
    def _():
        wait_for(ezr.at[0 : NZ - 1], ZS)
        for q in range(NP - 1):
            wait_for(yr.at[0], YS)

    @pl.when(jnp.logical_not(worker))
    def _():
        wait_for(wg.at[0:3], WAS)
        wait_for(wz, WBS)

    @pl.when(worker)
    def _():
        wait_for(wc, W0S)
        wait_for(ezr.at[0 : NZ - 1], ES)
        wait_for(part.at[0:3], KS)
        wait_for(kp.at[0:3], PS)

        @pl.when(lead)
        def _():
            wait_for(full.at[0:3], FS)

        @pl.when(jnp.logical_not(lead))
        def _():
            wait_for(kp.at[0], PS)


PARTS = 6


def look_up_kernel(
    table, keys, step, tokens,
    master_out, one_out, two_out, section_input, section_keys,
    table_v, keys_v, step_v, tokens_v, rows_v, looked, looked_keys, sem,
):
    lead = lax.axis_index("pipe") == 1
    width = D // PARTS

    def move(src, dst, which):
        copy = pltpu.make_async_copy(src, dst, sem.at[which])
        copy.start()
        return copy

    def give(part):
        lanes = slice(part * width, (part + 1) * width)
        return move(looked.at[:, lanes], section_input.at[:, lanes], part)

    load_step = move(step, step_v, 6)

    @pl.when(lead)
    def _():
        load_tokens = move(tokens, tokens_v, 7)
        load_table = move(table, table_v, 8)
        load_keys = move(keys, keys_v, 9)
        load_tokens.wait()
        rows = lax.broadcasted_iota(jnp.int32, (NX * NZ, tokens_v.shape[1]), 0)
        hot = jnp.where(rows == tokens_v[...], 1.0, 0.0).T.astype(jnp.bfloat16)
        load_table.wait()
        gives = []
        for part in range(PARTS):
            lanes = slice(part * width, (part + 1) * width)
            columns = table_v[:, :, lanes].reshape(NX * NZ, width)
            looked[:, lanes] = jnp.dot(
                hot, columns, preferred_element_type=jnp.float32
            ).astype(jnp.bfloat16)
            gives.append(give(part))
        load_keys.wait()
        looked_keys[...] = jnp.dot(
            hot, keys_v[...], preferred_element_type=jnp.float32
        ).astype(jnp.bfloat16)
        gives.append(move(looked_keys, section_keys, 10))
        for copy in gives:
            copy.wait()

    @pl.when(jnp.logical_not(lead))
    def _():
        looked[...] = jnp.zeros_like(looked)
        looked_keys[...] = jnp.zeros_like(looked_keys)
        gives = [give(part) for part in range(PARTS)]
        gives.append(move(looked_keys, section_keys, 10))
        for copy in gives:
            copy.wait()

    load_step.wait()
    for j in range(NCH):
        lanes = slice(j * LANES, (j + 1) * LANES)
        for k in range(3):
            rows_v[k, :, lanes] = step_v[k, j : j + 1, :]
    outs = [
        move(rows_v.at[k], out, 11 + k) for k, out in enumerate((master_out, one_out, two_out))
    ]
    for copy in outs:
        copy.wait()


def shards(
    grad_partials, master, moment_one, moment_two, token_rows, input_gain, key_weight, key_gain
):
    rows, kvw, count = NX * NZ, NP * HEAD_DIM, token_rows.shape[0]
    bf16, f32 = jnp.bfloat16, jnp.float32
    hbm = pl.BlockSpec(memory_space=pl.ANY)
    table, keys, step = pl.pallas_call(
        comm_kernel,
        out_shape=(
            jax.ShapeDtypeStruct((NX, NZ, D), bf16),
            jax.ShapeDtypeStruct((rows, kvw), bf16),
            jax.ShapeDtypeStruct((3, PAD, LANES), f32),
        ),
        in_specs=[hbm] * 7,
        out_specs=(hbm,) * 3,
        scratch_shapes=[
            pltpu.VMEM((NX, NZ, D), bf16),
            pltpu.VMEM((NZ * PAD, LANES), f32),
            pltpu.VMEM((NZ, PAD, LANES), bf16),
            pltpu.VMEM((2 * REACH, PAD, LANES), bf16),
            pltpu.VMEM((REACH, PAD, LANES), bf16),
            pltpu.VMEM((REACH - 1, PAD, LANES), bf16),
            pltpu.VMEM((2, PAD, LANES), bf16),
            pltpu.VMEM((2, PAD, LANES), f32),
            pltpu.VMEM((3, 1, D), f32),
            pltpu.VMEM((3, PAD, LANES), f32),
            pltpu.VMEM((PAD, LANES), bf16),
            pltpu.VMEM((NZ, PAD, LANES), bf16),
            pltpu.VMEM((NZ * PAD, LANES), f32),
            pltpu.VMEM((NZ, D), bf16),
            pltpu.VMEM((NX, NZ, D), bf16),
            pltpu.VMEM((NX, NZ, KW), bf16),
            pltpu.VMEM((WROWS, LANES), bf16),
            pltpu.VMEM((WPAD, LANES), bf16),
            pltpu.VMEM((WPAD, HEADS2), bf16),
            pltpu.VMEM((4, WPAD, HEADS2), bf16),
            pltpu.VMEM((4, 4, WPAD, HEADS2), bf16),
            pltpu.VMEM((WPAD, LANES), f32),
            pltpu.VMEM((KW, HEADS2), bf16),
            pltpu.VMEM((NX * NP // 2, rows, HEADS2), bf16),
            pltpu.VMEM((NCH, LANES), f32),
            pltpu.VMEM((1, D), f32),
            pltpu.VMEM((1, HEAD_DIM), f32),
            pltpu.VMEM((3, PAD, LANES), f32),
            pltpu.VMEM((rows, kvw), bf16),
            pltpu.SemaphoreType.DMA((39,)),
        ],
        compiler_params=pltpu.CompilerParams(
            collective_id=0, has_side_effects=True, vmem_limit_bytes=VMEM_BYTES
        ),
        name="sum_step_gather",
    )(
        grad_partials, master, moment_one, moment_two, key_weight,
        input_gain.reshape(NCH, LANES), key_gain.reshape(1, HEAD_DIM),
    )
    line = jax.ShapeDtypeStruct((1, D), f32)
    new_master, new_one, new_two, section_input, section_keys = pl.pallas_call(
        look_up_kernel,
        out_shape=(
            line, line, line,
            jax.ShapeDtypeStruct((count, D), bf16),
            jax.ShapeDtypeStruct((count, kvw), bf16),
        ),
        in_specs=[hbm] * 4,
        out_specs=(hbm,) * 5,
        scratch_shapes=[
            pltpu.VMEM((NX, NZ, D), bf16),
            pltpu.VMEM((rows, kvw), bf16),
            pltpu.VMEM((3, PAD, LANES), f32),
            pltpu.VMEM((1, count), jnp.int32),
            pltpu.VMEM((3, 1, D), f32),
            pltpu.VMEM((count, D), bf16),
            pltpu.VMEM((count, kvw), bf16),
            pltpu.SemaphoreType.DMA((14,)),
        ],
        compiler_params=pltpu.CompilerParams(vmem_limit_bytes=VMEM_BYTES),
        name="look_up",
    )(table, keys, step, token_rows.reshape(1, count))
    return new_master, new_one, new_two, section_input[None], section_keys[None]


def solution(mesh):
    in_specs = (
        P("pipe", "dp", None, None),
        P("dp", None),
        P("dp", None),
        P("dp", None),
        P("dp"),
        P(),
        P("dp", "pipe"),
        P(),
    )
    out_specs = (
        P("dp", None),
        P("dp", None),
        P("dp", None),
        P("pipe", "dp", None),
        P("pipe", "dp", None),
    )
    return jax.shard_map(shards, mesh=mesh, in_specs=in_specs, out_specs=out_specs, check_vma=False)
```

```python
import jax
import jax.numpy as jnp
from jax import lax
from jax.experimental import pallas as pl
from jax.experimental.pallas import tpu as pltpu
from jax.sharding import PartitionSpec as P

MESH = pl.DeviceIdType.MESH
HEAD_DIM = 128
LANES = 128
NX, NZ, NP = 4, 16, 8
D = 5376
NCH = D // LANES
PAD = 48
WROWS = 84
WPAD = 96
KC = 11
KW = KC * LANES
HEADS2 = 2 * HEAD_DIM
VMEM_BYTES = 60 * 2**20
SHARES = {1: slice(0, 2688), 3: slice(2688, 4096), 6: slice(4096, D)}

(
    XS, ZS, YS, YR0, YR1, W0S, W0R, WAS, WB,
    ES, EM, EP, ER, KS, KR, FS, FR, PS, PR, LM, L1, L2, LW, LG, LK, O1, O2, O3, XR,
) = range(29)
THIRDS, BAND = 3, 14
ZR, RP, RM, WR = XR + THIRDS, XR + 2 * THIRDS, XR + 3 * THIRDS, XR + 4 * THIRDS
SEMS = WR + NZ
REACH = 4


def place(j):
    return j // BAND * 16 + j % BAND


def first_chunk(x):
    return (x // 2) * 21 + lax.rem(x, 2) * 10


def comm_kernel(
    grad, master, moment_one, moment_two, weight, gain, key_gain,
    table_out, keys_out, step_out,
    gx, zs, zb, zr, zp, zm, zq, yr, state, prior, erow, ezr, ef, block, full, part, wv, wc, wp, hz, wz, wf, wk, kp,
    gv, gl, kg, step, keys, sem,
):
    dp = lax.axis_index("dp")
    pipe = lax.axis_index("pipe")
    x, z = dp // NZ, lax.rem(dp, NZ)
    y = pipe // 2
    far = y == NP // 2 - 1
    worker = jnp.where(far, 2 * y, 2 * y + 1) == pipe
    mate = jnp.where(lax.rem(pipe, 2) == 0, pipe + 1, pipe - 1)
    source = jnp.logical_or(pipe == 0, pipe == NP - 1)
    lead, last = pipe == 1, pipe == NP - 2
    reducer = jnp.logical_or(lead, last)

    def at(x_to, z_to, pipe_to):
        return (x_to * NZ + z_to, pipe_to)

    def send(src, dst, sent, arrived, where):
        pltpu.make_async_remote_copy(
            src_ref=src, dst_ref=dst, send_sem=sem.at[sent], recv_sem=sem.at[arrived],
            device_id=where, device_id_type=MESH,
        ).start()

    def wait_for(like, which):
        pltpu.make_async_copy(like, like, sem.at[which]).wait()

    barrier = pltpu.get_barrier_semaphore()

    def tell(where):
        pl.semaphore_signal(barrier, inc=1, device_id=where, device_id_type=MESH)

    def away(k):
        return lax.rem(z + k + NZ, NZ)

    near = [k for k in range(-REACH, REACH + 1) if k]

    @pl.when(worker)
    def _():
        for k in near:
            tell(at(x, away(k), pipe))
        for k in range(1, NX):
            tell(at(lax.rem(x + k, NX), z, pipe))
        tell((dp, mate))

    @pl.when(reducer)
    def _():
        for k in range(1, NX):
            tell(at(lax.rem(x + k, NX), z, mate))

    @pl.when(jnp.logical_not(worker))
    def _():
        tell(at(x, away(1), pipe))
        tell(at(x, away(-1), pipe))

    @pl.when(jnp.logical_or(pipe == 2, pipe == 4))
    def _():
        tell((dp, mate))

    @pl.when(jnp.logical_not(lead))
    def _():
        tell((dp, 1))

    @pl.when(jnp.logical_not(last))
    def _():
        tell((dp, NP - 2))

    @pl.when(lead)
    def _():
        for k in range(NX):
            for q in (3, 5, 6):
                if k > 0 or q != 6:
                    tell(at(lax.rem(x + k, NX), z, q))

    def load(src, dst, which):
        copy = pltpu.make_async_copy(src, dst, sem.at[which])
        copy.start()
        return copy

    load_weight = load(weight, wv, LW)
    load_state = [
        load(master, state.at[0], LM), load(moment_one, state.at[1], L1),
        load(moment_two, state.at[2], L2),
    ]
    load_gain = load(gain, gv, LG)
    load_key_gain = load(key_gain, kg, LK)

    peers = len(near) + NX - 1
    counts = {
        0: 3 + NX - 1, NP - 1: 3 + NX - 1, 2: 3, 4: 3,
        1: peers + NP - 1, 6: peers + NP - 1 + NX - 1, 3: peers + NX + 1, 5: peers + NX + 1,
    }
    for q, count in counts.items():

        @pl.when(pipe == q)
        def _(count=count):
            pl.semaphore_wait(barrier, count)

    @pl.when(source)
    def _():
        for band in range(THIRDS):
            lanes = slice(band * BAND * LANES, (band + 1) * BAND * LANES)
            for k in (2, 1, 3, 0):
                to = lax.rem(x + k, NX)
                rows = pl.ds(pl.multiple_of(to * NZ, NZ), NZ)
                send(
                    grad.at[0, 0, rows, lanes], gx.at[x, :, lanes], XS, XR + band,
                    at(to, z, mate),
                )

    load_weight.wait()
    wc[...] = jnp.zeros_like(wc)
    wide = wv[...].astype(jnp.float32)
    for q in range(4):
        @pl.when(lax.rem(z, 4) == q)
        def _(q=q):
            wf[...] = jnp.zeros_like(wf)
            wf[4 * q : 4 * q + WROWS, :] = wide
            wc[...] = wf[...].astype(jnp.bfloat16)

    for high in (False, True):
        lanes = slice(LANES, HEADS2) if high else slice(0, LANES)

        @pl.when((lax.rem(pipe, 2) == 1) == high)
        def _(lanes=lanes):
            @pl.when(worker)
            def _():
                send(wc, wp.at[:, lanes], W0S, W0R, (dp, mate))

            @pl.when(jnp.logical_not(worker))
            def _():
                wp[:, lanes] = wc[...]

    def weights_round(step, away_step, count):
        row = away(step)
        if abs(step) < count:
            send(hz.at[row], hz.at[row], WAS, WR + away_step, at(x, away(-1 if step > 0 else 1), pipe))
        send(hz.at[row], wz.at[lax.rem(row, 4), row // 4], WAS, WB, (dp, mate))

    @pl.when(jnp.logical_not(worker))
    def _():
        wait_for(wc, W0R)
        hz[z] = wp[...]
        send(hz.at[z], hz.at[z], WAS, WR, at(x, away(1), pipe))
        send(hz.at[z], hz.at[z], WAS, WR + 8, at(x, away(-1), pipe))
        send(hz.at[z], wz.at[lax.rem(z, 4), z // 4], WAS, WB, (dp, mate))
        for step in range(1, 9):
            wait_for(wp, WR + step - 1)
            weights_round(-step, step, 8)
            if step < 8:
                wait_for(wp, WR + 8 + step - 1)
                weights_round(step, 8 + step, 7)

    prior[...] = jnp.zeros_like(prior)
    for copy in load_state:
        copy.wait()
    for j in range(NCH):
        lanes = slice(j * LANES, (j + 1) * LANES)
        for k in range(3):
            prior[k, place(j) : place(j) + 1, :] = state[k, :, lanes]

    load_gain.wait()
    load_key_gain.wait()

    def weights_join():
        wait_for(wz, WB)
        side = lax.rem(x, 2)
        spare = pl.multiple_of((1 - side) * NZ * WROWS, 64)
        wk[pl.ds(spare, 64), :] = jnp.zeros((64, HEADS2), jnp.bfloat16)
        for g in range(4):
            start = pl.multiple_of(side * 64 + g * 4 * WROWS, 16)

            def put(row, value):
                wk[pl.ds(pl.multiple_of(start + row, 16), value.shape[0]), :] = value

            for k in range(4):
                edge = wz[k, g, 0:16, :]
                if k:
                    edge = edge + wz[k - 1, g, 80:96, :]
                put(80 * k, edge)
                put(80 * k + 16, wz[k, g, 16:80, :])
            put(320, wz[3, g, 80:96, :])
        for j in range(NCH):
            gl[:, j * LANES : (j + 1) * LANES] = gv[j : j + 1, :]

    def row_sum(refs):
        total = refs[0].astype(jnp.float32)
        for ref in refs[1:]:
            total = total + ref.astype(jnp.float32)
        return total

    @pl.when(reducer)
    def _():
        zs[...] = jnp.zeros_like(zs)
        for band in range(THIRDS):
            wait_for(gx.at[:, :, 0 : BAND * LANES], XR + band)
            for j in range(band * BAND, (band + 1) * BAND):
                lanes = slice(j * LANES, (j + 1) * LANES)
                total = row_sum([gx[k, :, lanes] for k in range(NX)])
                zs[pl.ds(place(j), NZ, stride=PAD), :] = total
            part_rows = slice(16 * band, 16 * (band + 1))
            for k in range(NZ):
                zb[k, part_rows, :] = zs[
                    PAD * k + 16 * band : PAD * k + 16 * (band + 1), :
                ].astype(jnp.bfloat16)

            def give(row, dst, arrived, k, part_rows=part_rows, band=band):
                send(
                    zb.at[row, part_rows], dst.at[part_rows], ZS, arrived + band,
                    at(x, away(k), pipe),
                )

            for k in range(REACH, 0, -1):
                give(away(k + REACH), zp.at[k - 1], RP, k)
                if k < REACH:
                    give(away(-k - REACH), zm.at[k - 1], RM, -k)
            for k in range(1, REACH):
                give(away(k), zr.at[REACH - k], ZR, k)
                give(away(-k), zr.at[REACH + k - 1], ZR, -k)

        for band in range(THIRDS):
            part_rows = slice(16 * band, 16 * (band + 1))
            ways = (
                (zp, RP, REACH, 0, 0),
                (zm, RM, REACH - 1, 1, 2 * REACH - 1),
            )
            for ref, arrived, count, slot, there in ways:
                k = REACH if slot == 0 else -REACH
                wait_for(ref.at[0:count, part_rows], arrived + band)
                own = zs[pl.ds(pl.multiple_of(away(k) * PAD + 16 * band, 16), 16), :]
                passed = own + row_sum([ref[q, part_rows, :] for q in range(count)])
                zq[slot, part_rows, :] = passed.astype(jnp.bfloat16)
                send(
                    zq.at[slot, part_rows], zr.at[there, part_rows], ZS, ZR + band,
                    at(x, away(k), pipe),
                )

        for band in range(THIRDS):
            wait_for(zr.at[:, 0:16], ZR + band)
        own = zs[pl.ds(pl.multiple_of(z * PAD, PAD), PAD), :]
        total = own + row_sum([zr[k] for k in range(2 * REACH)])

        @pl.when(lead)
        def _():
            yr[0] = total
            for q in (3, 5, 6, 0, 2, 4, 7):
                send(yr.at[0], yr.at[0], YS, YR0, (dp, q))

        @pl.when(last)
        def _():
            yr[1] = total
            for q in (1, 3, 5, 0, 2, 4, 7):
                send(yr.at[1], yr.at[1], YS, YR1, (dp, q))

    @pl.when(jnp.logical_not(lead))
    def _():
        wait_for(yr.at[0], YR0)

    @pl.when(jnp.logical_not(last))
    def _():
        wait_for(yr.at[1], YR1)

    gradient = yr[0] + yr[1]
    new_one = 0.9 * prior[1] + 0.1 * gradient
    new_two = 0.95 * prior[2] + 0.05 * gradient * gradient
    correct_one = 1.0 - 0.9**10
    correct_two = 1.0 - 0.95**10
    update = new_one / correct_one / (jnp.sqrt(new_two / correct_two) + 1e-08)
    new_master = prior[0] - 0.001 * update
    step[0] = new_master
    step[1] = new_one
    step[2] = new_two
    keep = pltpu.make_async_copy(step, step_out, sem.at[O1])

    @pl.when(worker)
    def _():
        table = new_master.astype(jnp.bfloat16).astype(jnp.float32)
        erow[...] = (table * jnp.float32(D**0.5)).astype(jnp.bfloat16)
        for k in (4, -4, 3, -3, 2, -2, 1, -1):
            arrives = {REACH: EM, -REACH: EP}.get(k, ER)
            send(erow, ezr.at[z], ES, arrives, at(x, away(k), pipe))
        ezr[z] = erow[...]

    keep.start()

    @pl.when(worker)
    def _():
        def pass_up():
            wait_for(erow, EM)
            row = away(-REACH)
            for k in range(REACH, 0, -1):
                send(ezr.at[row], ezr.at[row], ES, ER, at(x, away(k), pipe))

        def pass_down():
            wait_for(erow, EP)
            row = away(REACH)
            for k in range(REACH - 1, 0, -1):
                send(ezr.at[row], ezr.at[row], ES, ER, at(x, away(-k), pipe))

        @pl.when(z < NZ // 2)
        def _():
            pass_down()
            pass_up()

        @pl.when(z >= NZ // 2)
        def _():
            pass_up()
            pass_down()

        weights_join()

        wait_for(ezr.at[0 : NZ - 3], ER)
        ef[...] = ezr[...].astype(jnp.float32).reshape(NZ * PAD, LANES)

        for j in range(NCH):
            lanes = slice(j * LANES, (j + 1) * LANES)
            block[:, lanes] = ef[pl.ds(place(j), NZ, stride=PAD), :].astype(jnp.bfloat16)

        def features(x_of):
            return pl.ds(pl.multiple_of(first_chunk(x_of) * LANES, LANES), KW)

        for k in range(1, NX):
            to = lax.rem(x + k, NX)
            send(block.at[:, features(to)], part.at[x], KS, KR, at(to, z, pipe))

        for q, lanes in SHARES.items():

            @pl.when(pipe == q)
            def _(lanes=lanes):
                for k in range(1, NX):
                    to = at(lax.rem(x + k, NX), z, 1)
                    send(block.at[:, lanes], full.at[x, :, lanes], FS, FR, to)

        @pl.when(lead)
        def _():
            full[x] = block[...]

        part[x] = block[:, features(x)]
        wait_for(part.at[0:3], KR)
        scaled = part[...].reshape(NX * NZ, KW).astype(jnp.float32) * gl[:, features(x)]
        product = jnp.dot(
            scaled.astype(jnp.bfloat16), wk[...], preferred_element_type=jnp.float32
        )
        slot = y * NX + x
        kp[slot] = product.astype(jnp.bfloat16)
        for k in range(NX):
            to = lax.rem(x + k, NX)

            def share(to=to):
                send(kp.at[slot], kp.at[slot], PS, PR, at(to, z, 1))

            if k:
                share()
            else:
                pl.when(jnp.logical_not(lead))(share)

    @pl.when(lead)
    def _():
        wait_for(full.at[0:3], FR)
        out = pltpu.make_async_copy(full, table_out, sem.at[O2])
        out.start()
        squares = jnp.zeros((NX * NZ, LANES), jnp.float32)
        for j in range(NCH):
            wide = full[:, :, LANES * j : LANES * (j + 1)].astype(jnp.float32)
            wide = wide.reshape(NX * NZ, LANES)
            squares = squares + wide * wide
        scale = lax.rsqrt(jnp.sum(squares, axis=-1, keepdims=True) / D + 1e-06)
        wait_for(kp.at[0 : NX * NP // 2 - 1], PR)
        for s in range(NP // 2):
            raw = kp[s * NX].astype(jnp.float32)
            for k in range(1, NX):
                raw = raw + kp[s * NX + k].astype(jnp.float32)
            raw = raw * scale
            for h in range(2):
                head = raw[:, h * HEAD_DIM : (h + 1) * HEAD_DIM]
                mean = jnp.mean(head * head, axis=-1, keepdims=True)
                first = s * HEADS2 + h * HEAD_DIM
                keys[:, first : first + HEAD_DIM] = (
                    head * lax.rsqrt(mean + 1e-06) * kg[...]
                ).astype(jnp.bfloat16)
        last_out = pltpu.make_async_copy(keys, keys_out, sem.at[O3])
        last_out.start()
        out.wait()
        last_out.wait()

    keep.wait()

    @pl.when(source)
    def _():
        wait_for(gx, XS)

    @pl.when(reducer)
    def _():
        wait_for(ezr.at[0 : NZ - 1], ZS)
        for q in range(NP - 1):
            wait_for(yr.at[0], YS)

    @pl.when(jnp.logical_not(worker))
    def _():
        wait_for(hz, WAS)
        wait_for(hz.at[0 : NZ - 1], WAS)

    @pl.when(worker)
    def _():
        wait_for(wc, W0S)
        wait_for(ezr.at[0 : NZ - 1], ES)
        wait_for(part.at[0:3], KS)
        wait_for(kp.at[0:3], PS)

        for q, lanes in SHARES.items():

            @pl.when(pipe == q)
            def _(lanes=lanes):
                wait_for(full.at[0 : NX - 1, :, lanes], FS)

        @pl.when(jnp.logical_not(lead))
        def _():
            wait_for(kp.at[0], PS)


PARTS = 6


def look_up_kernel(
    table, keys, step, tokens,
    master_out, one_out, two_out, section_input, section_keys,
    table_v, keys_v, step_v, tokens_v, rows_v, looked, looked_keys, sem,
):
    lead = lax.axis_index("pipe") == 1
    width = D // PARTS

    def move(src, dst, which):
        copy = pltpu.make_async_copy(src, dst, sem.at[which])
        copy.start()
        return copy

    def give(part):
        lanes = slice(part * width, (part + 1) * width)
        return move(looked.at[:, lanes], section_input.at[:, lanes], part)

    load_step = move(step, step_v, 6)

    @pl.when(lead)
    def _():
        load_tokens = move(tokens, tokens_v, 7)
        load_table = move(table, table_v, 8)
        load_keys = move(keys, keys_v, 9)
        load_tokens.wait()
        rows = lax.broadcasted_iota(jnp.int32, (NX * NZ, tokens_v.shape[1]), 0)
        hot = jnp.where(rows == tokens_v[...], 1.0, 0.0).T.astype(jnp.bfloat16)
        load_table.wait()
        gives = []
        for part in range(PARTS):
            lanes = slice(part * width, (part + 1) * width)
            columns = table_v[:, :, lanes].reshape(NX * NZ, width)
            looked[:, lanes] = jnp.dot(
                hot, columns, preferred_element_type=jnp.float32
            ).astype(jnp.bfloat16)
            gives.append(give(part))
        load_keys.wait()
        looked_keys[...] = jnp.dot(
            hot, keys_v[...], preferred_element_type=jnp.float32
        ).astype(jnp.bfloat16)
        gives.append(move(looked_keys, section_keys, 10))
        for copy in gives:
            copy.wait()

    @pl.when(jnp.logical_not(lead))
    def _():
        looked[...] = jnp.zeros_like(looked)
        looked_keys[...] = jnp.zeros_like(looked_keys)
        gives = [give(part) for part in range(PARTS)]
        gives.append(move(looked_keys, section_keys, 10))
        for copy in gives:
            copy.wait()

    load_step.wait()
    for j in range(NCH):
        lanes = slice(j * LANES, (j + 1) * LANES)
        for k in range(3):
            rows_v[k, :, lanes] = step_v[k, place(j) : place(j) + 1, :]
    outs = [
        move(rows_v.at[k], out, 11 + k) for k, out in enumerate((master_out, one_out, two_out))
    ]
    for copy in outs:
        copy.wait()


def shards(
    grad_partials, master, moment_one, moment_two, token_rows, input_gain, key_weight, key_gain
):
    rows, kvw, count = NX * NZ, NP * HEAD_DIM, token_rows.shape[0]
    bf16, f32 = jnp.bfloat16, jnp.float32
    hbm = pl.BlockSpec(memory_space=pl.ANY)
    table, keys, step = pl.pallas_call(
        comm_kernel,
        out_shape=(
            jax.ShapeDtypeStruct((NX, NZ, D), bf16),
            jax.ShapeDtypeStruct((rows, kvw), bf16),
            jax.ShapeDtypeStruct((3, PAD, LANES), f32),
        ),
        in_specs=[hbm] * 7,
        out_specs=(hbm,) * 3,
        scratch_shapes=[
            pltpu.VMEM((NX, NZ, D), bf16),
            pltpu.VMEM((NZ * PAD, LANES), f32),
            pltpu.VMEM((NZ, PAD, LANES), bf16),
            pltpu.VMEM((2 * REACH, PAD, LANES), bf16),
            pltpu.VMEM((REACH, PAD, LANES), bf16),
            pltpu.VMEM((REACH - 1, PAD, LANES), bf16),
            pltpu.VMEM((2, PAD, LANES), bf16),
            pltpu.VMEM((2, PAD, LANES), f32),
            pltpu.VMEM((3, 1, D), f32),
            pltpu.VMEM((3, PAD, LANES), f32),
            pltpu.VMEM((PAD, LANES), bf16),
            pltpu.VMEM((NZ, PAD, LANES), bf16),
            pltpu.VMEM((NZ * PAD, LANES), f32),
            pltpu.VMEM((NZ, D), bf16),
            pltpu.VMEM((NX, NZ, D), bf16),
            pltpu.VMEM((NX, NZ, KW), bf16),
            pltpu.VMEM((WROWS, LANES), bf16),
            pltpu.VMEM((WPAD, LANES), bf16),
            pltpu.VMEM((WPAD, HEADS2), bf16),
            pltpu.VMEM((NZ, WPAD, HEADS2), bf16),
            pltpu.VMEM((4, 4, WPAD, HEADS2), bf16),
            pltpu.VMEM((WPAD, LANES), f32),
            pltpu.VMEM((KW, HEADS2), bf16),
            pltpu.VMEM((NX * NP // 2, rows, HEADS2), bf16),
            pltpu.VMEM((NCH, LANES), f32),
            pltpu.VMEM((1, D), f32),
            pltpu.VMEM((1, HEAD_DIM), f32),
            pltpu.VMEM((3, PAD, LANES), f32),
            pltpu.VMEM((rows, kvw), bf16),
            pltpu.SemaphoreType.DMA((SEMS,)),
        ],
        compiler_params=pltpu.CompilerParams(
            collective_id=0, has_side_effects=True, vmem_limit_bytes=VMEM_BYTES
        ),
        name="sum_step_gather",
    )(
        grad_partials, master, moment_one, moment_two, key_weight,
        input_gain.reshape(NCH, LANES), key_gain.reshape(1, HEAD_DIM),
    )
    line = jax.ShapeDtypeStruct((1, D), f32)
    new_master, new_one, new_two, section_input, section_keys = pl.pallas_call(
        look_up_kernel,
        out_shape=(
            line, line, line,
            jax.ShapeDtypeStruct((count, D), bf16),
            jax.ShapeDtypeStruct((count, kvw), bf16),
        ),
        in_specs=[hbm] * 4,
        out_specs=(hbm,) * 5,
        scratch_shapes=[
            pltpu.VMEM((NX, NZ, D), bf16),
            pltpu.VMEM((rows, kvw), bf16),
            pltpu.VMEM((3, PAD, LANES), f32),
            pltpu.VMEM((1, count), jnp.int32),
            pltpu.VMEM((3, 1, D), f32),
            pltpu.VMEM((count, D), bf16),
            pltpu.VMEM((count, kvw), bf16),
            pltpu.SemaphoreType.DMA((14,)),
        ],
        compiler_params=pltpu.CompilerParams(vmem_limit_bytes=VMEM_BYTES),
        name="look_up",
    )(table, keys, step, token_rows.reshape(1, count))
    return new_master, new_one, new_two, section_input[None], section_keys[None]


def solution(mesh):
    in_specs = (
        P("pipe", "dp", None, None),
        P("dp", None),
        P("dp", None),
        P("dp", None),
        P("dp"),
        P(),
        P("dp", "pipe"),
        P(),
    )
    out_specs = (
        P("dp", None),
        P("dp", None),
        P("dp", None),
        P("pipe", "dp", None),
        P("pipe", "dp", None),
    )
    return jax.shard_map(shards, mesh=mesh, in_specs=in_specs, out_specs=out_specs, check_vma=False)
```

```python
import jax
import jax.numpy as jnp
from jax import lax
from jax.experimental import pallas as pl
from jax.experimental.pallas import tpu as pltpu
from jax.sharding import PartitionSpec as P

MESH = pl.DeviceIdType.MESH
HEAD_DIM = 128
LANES = 128
NX, NZ, NP = 4, 16, 8
D = 5376
NCH = D // LANES
PAD = 48
WROWS = 84
WPAD = 96
KC = 11
KW = KC * LANES
HEADS2 = 2 * HEAD_DIM
VMEM_BYTES = 60 * 2**20
SHARES = {1: slice(0, 2688), 3: slice(2688, 4096), 7: slice(4096, D)}

(
    XS, ZS, YS, YR0, YR1, W0S, W0R, WAS, WB,
    ES, EM, EP, ER, KS, KR, FS, FR, PS, PR, LM, L1, L2, LW, LG, LK, O1, O2, O3, XR,
) = range(29)
THIRDS, BAND = 3, 14
ZR, RP, RM, WR = XR + THIRDS, XR + 2 * THIRDS, XR + 3 * THIRDS, XR + 4 * THIRDS
SEMS = WR + NZ
REACH = 4


def place(j):
    return j // BAND * 16 + j % BAND


def first_chunk(x):
    return (x // 2) * 21 + lax.rem(x, 2) * 10


def comm_kernel(
    grad, master, moment_one, moment_two, weight, gain, key_gain,
    table_out, keys_out, step_out,
    gx, zs, zb, zr, zp, zm, zq, yr, state, prior, erow, ezr, ef, block, full, part, wv, wc, wp, hz, wz, wf, wk, kp,
    gv, gl, kg, step, keys, sem,
):
    dp = lax.axis_index("dp")
    pipe = lax.axis_index("pipe")
    x, z = dp // NZ, lax.rem(dp, NZ)
    y = pipe // 2
    worker = lax.rem(pipe, 2) == 1
    mate = jnp.where(worker, pipe - 1, pipe + 1)
    lead, last = pipe == 1, pipe == NP - 1
    reducer = jnp.logical_or(lead, last)

    def at(x_to, z_to, pipe_to):
        return (x_to * NZ + z_to, pipe_to)

    def send(src, dst, sent, arrived, where):
        pltpu.make_async_remote_copy(
            src_ref=src, dst_ref=dst, send_sem=sem.at[sent], recv_sem=sem.at[arrived],
            device_id=where, device_id_type=MESH,
        ).start()

    def wait_for(like, which):
        pltpu.make_async_copy(like, like, sem.at[which]).wait()

    barrier = pltpu.get_barrier_semaphore()

    def tell(where):
        pl.semaphore_signal(barrier, inc=1, device_id=where, device_id_type=MESH)

    def away(k):
        return lax.rem(z + k + NZ, NZ)

    near = [k for k in range(-REACH, REACH + 1) if k]

    @pl.when(worker)
    def _():
        for k in near:
            tell(at(x, away(k), pipe))
        for k in range(1, NX):
            tell(at(lax.rem(x + k, NX), z, pipe))
        tell((dp, mate))

    @pl.when(lead)
    def _():
        for k in range(1, NX):
            tell(at(lax.rem(x + k, NX), z, 0))

    @pl.when(jnp.logical_not(worker))
    def _():
        for k in (1, -1, 2, -2):
            tell(at(x, away(k), pipe))

    @pl.when(jnp.logical_or(pipe == 2, pipe == 4))
    def _():
        tell((dp, mate))

    @pl.when(jnp.logical_not(lead))
    def _():
        tell((dp, 1))

    @pl.when(jnp.logical_not(last))
    def _():
        tell((dp, NP - 1))

    @pl.when(lead)
    def _():
        for k in range(NX):
            for q in (3, 5, 7):
                if k > 0 or q != 7:
                    tell(at(lax.rem(x + k, NX), z, q))

    def load(src, dst, which):
        copy = pltpu.make_async_copy(src, dst, sem.at[which])
        copy.start()
        return copy

    load_weight = load(weight, wv, LW)
    load_state = [
        load(master, state.at[0], LM), load(moment_one, state.at[1], L1),
        load(moment_two, state.at[2], L2),
    ]
    load_gain = load(gain, gv, LG)
    load_key_gain = load(key_gain, kg, LK)

    peers = len(near) + NX - 1
    counts = {
        0: 5 + NX - 1, 2: 5, 4: 5, 6: 5,
        1: peers + NP - 1, 7: peers + NP - 1 + NX - 1, 3: peers + NX + 1, 5: peers + NX + 1,
    }
    for q, count in counts.items():

        @pl.when(pipe == q)
        def _(count=count):
            pl.semaphore_wait(barrier, count)

    for here in (0, NP - 1):

        @pl.when(pipe == here)
        def _(here=here):
            for band in range(THIRDS):
                lanes = slice(band * BAND * LANES, (band + 1) * BAND * LANES)
                for k in (2, 1, 3, 0):
                    to = lax.rem(x + k, NX)
                    rows = pl.ds(pl.multiple_of(to * NZ, NZ), NZ)
                    src, dst = grad.at[0, 0, rows, lanes], gx.at[x, :, lanes]
                    if here and not k:
                        load(src, dst, XR + band)
                    else:
                        send(src, dst, XS, XR + band, at(to, z, 1 if here == 0 else here))

    load_weight.wait()
    wc[...] = jnp.zeros_like(wc)
    wide = wv[...].astype(jnp.float32)
    for q in range(4):
        @pl.when(lax.rem(z, 4) == q)
        def _(q=q):
            wf[...] = jnp.zeros_like(wf)
            wf[4 * q : 4 * q + WROWS, :] = wide
            wc[...] = wf[...].astype(jnp.bfloat16)

    @pl.when(worker)
    def _():
        send(wc, wp.at[:, LANES:HEADS2], W0S, W0R, (dp, mate))

    @pl.when(jnp.logical_not(worker))
    def _():
        wp[:, 0:LANES] = wc[...]

    def weights_on(way, step):
        row, first, limit = away(-way * step), (WR if way > 0 else WR + 8), (8 if way > 0 else 7)
        if step % 2 == 0:
            for k in (2, 1):
                if step + k <= limit:
                    to = at(x, away(way * k), pipe)
                    send(hz.at[row], hz.at[row], WAS, first + step + k - 1, to)

    def weights_in(way, step):
        wait_for(wp, (WR if way > 0 else WR + 8) + step - 1)
        weights_on(way, step)
        row = away(-way * step)
        send(hz.at[row], wz.at[lax.rem(row, 4), row // 4], WAS, WB, (dp, mate))

    @pl.when(jnp.logical_not(worker))
    def _():
        wait_for(wc, W0R)
        hz[z] = wp[...]
        weights_on(1, 0)
        weights_on(-1, 0)
        send(hz.at[z], wz.at[lax.rem(z, 4), z // 4], WAS, WB, (dp, mate))
        for step in (2, 1, 4, 3, 6, 5, 8, 7):
            weights_in(1, step)
            if step < 8:
                weights_in(-1, step)

    prior[...] = jnp.zeros_like(prior)
    for copy in load_state:
        copy.wait()
    for j in range(NCH):
        lanes = slice(j * LANES, (j + 1) * LANES)
        for k in range(3):
            prior[k, place(j) : place(j) + 1, :] = state[k, :, lanes]

    load_gain.wait()
    load_key_gain.wait()

    def weights_join():
        wait_for(wz, WB)
        side = lax.rem(x, 2)
        spare = pl.multiple_of((1 - side) * NZ * WROWS, 64)
        wk[pl.ds(spare, 64), :] = jnp.zeros((64, HEADS2), jnp.bfloat16)
        for g in range(4):
            start = pl.multiple_of(side * 64 + g * 4 * WROWS, 16)

            def put(row, value):
                wk[pl.ds(pl.multiple_of(start + row, 16), value.shape[0]), :] = value

            for k in range(4):
                edge = wz[k, g, 0:16, :]
                if k:
                    edge = edge + wz[k - 1, g, 80:96, :]
                put(80 * k, edge)
                put(80 * k + 16, wz[k, g, 16:80, :])
            put(320, wz[3, g, 80:96, :])
        for j in range(NCH):
            gl[:, j * LANES : (j + 1) * LANES] = gv[j : j + 1, :]

    def row_sum(refs):
        total = refs[0].astype(jnp.float32)
        for ref in refs[1:]:
            total = total + ref.astype(jnp.float32)
        return total

    @pl.when(reducer)
    def _():
        zs[...] = jnp.zeros_like(zs)
        for band in range(THIRDS):
            wait_for(gx.at[:, :, 0 : BAND * LANES], XR + band)
            for j in range(band * BAND, (band + 1) * BAND):
                lanes = slice(j * LANES, (j + 1) * LANES)
                total = row_sum([gx[k, :, lanes] for k in range(NX)])
                zs[pl.ds(place(j), NZ, stride=PAD), :] = total
            part_rows = slice(16 * band, 16 * (band + 1))
            for k in range(NZ):
                zb[k, part_rows, :] = zs[
                    PAD * k + 16 * band : PAD * k + 16 * (band + 1), :
                ].astype(jnp.bfloat16)

            def give(row, dst, arrived, k, part_rows=part_rows, band=band):
                send(
                    zb.at[row, part_rows], dst.at[part_rows], ZS, arrived + band,
                    at(x, away(k), pipe),
                )

            for k in range(REACH, 0, -1):
                give(away(k + REACH), zp.at[k - 1], RP, k)
                if k < REACH:
                    give(away(-k - REACH), zm.at[k - 1], RM, -k)
            for k in range(1, REACH):
                give(away(k), zr.at[REACH - k], ZR, k)
                give(away(-k), zr.at[REACH + k - 1], ZR, -k)

        for band in range(THIRDS):
            part_rows = slice(16 * band, 16 * (band + 1))
            ways = (
                (zp, RP, REACH, 0, 0),
                (zm, RM, REACH - 1, 1, 2 * REACH - 1),
            )
            for ref, arrived, count, slot, there in ways:
                k = REACH if slot == 0 else -REACH
                wait_for(ref.at[0:count, part_rows], arrived + band)
                own = zs[pl.ds(pl.multiple_of(away(k) * PAD + 16 * band, 16), 16), :]
                passed = own + row_sum([ref[q, part_rows, :] for q in range(count)])
                zq[slot, part_rows, :] = passed.astype(jnp.bfloat16)
                send(
                    zq.at[slot, part_rows], zr.at[there, part_rows], ZS, ZR + band,
                    at(x, away(k), pipe),
                )

        for band in range(THIRDS):
            wait_for(zr.at[:, 0:16], ZR + band)
        own = zs[pl.ds(pl.multiple_of(z * PAD, PAD), PAD), :]
        total = own + row_sum([zr[k] for k in range(2 * REACH)])

        @pl.when(lead)
        def _():
            yr[0] = total
            for q in (3, 5, 7, 0, 2, 4, 6):
                send(yr.at[0], yr.at[0], YS, YR0, (dp, q))

        @pl.when(last)
        def _():
            yr[1] = total
            for q in (1, 3, 5, 0, 2, 4, 6):
                send(yr.at[1], yr.at[1], YS, YR1, (dp, q))

    @pl.when(jnp.logical_not(lead))
    def _():
        wait_for(yr.at[0], YR0)

    @pl.when(jnp.logical_not(last))
    def _():
        wait_for(yr.at[1], YR1)

    gradient = yr[0] + yr[1]
    new_one = 0.9 * prior[1] + 0.1 * gradient
    new_two = 0.95 * prior[2] + 0.05 * gradient * gradient
    correct_one = 1.0 - 0.9**10
    correct_two = 1.0 - 0.95**10
    update = new_one / correct_one / (jnp.sqrt(new_two / correct_two) + 1e-08)
    new_master = prior[0] - 0.001 * update
    step[0] = new_master
    step[1] = new_one
    step[2] = new_two
    keep = pltpu.make_async_copy(step, step_out, sem.at[O1])

    @pl.when(worker)
    def _():
        table = new_master.astype(jnp.bfloat16).astype(jnp.float32)
        erow[...] = (table * jnp.float32(D**0.5)).astype(jnp.bfloat16)
        for k in (4, -4, 3, -3, 2, -2, 1, -1):
            arrives = {REACH: EM, -REACH: EP}.get(k, ER)
            send(erow, ezr.at[z], ES, arrives, at(x, away(k), pipe))
        ezr[z] = erow[...]

    keep.start()

    @pl.when(worker)
    def _():
        def pass_up():
            wait_for(erow, EM)
            row = away(-REACH)
            for k in range(REACH, 0, -1):
                send(ezr.at[row], ezr.at[row], ES, ER, at(x, away(k), pipe))

        def pass_down():
            wait_for(erow, EP)
            row = away(REACH)
            for k in range(REACH - 1, 0, -1):
                send(ezr.at[row], ezr.at[row], ES, ER, at(x, away(-k), pipe))

        @pl.when(z < NZ // 2)
        def _():
            pass_down()
            pass_up()

        @pl.when(z >= NZ // 2)
        def _():
            pass_up()
            pass_down()

        weights_join()

        wait_for(ezr.at[0 : NZ - 3], ER)
        ef[...] = ezr[...].astype(jnp.float32).reshape(NZ * PAD, LANES)

        for j in range(NCH):
            lanes = slice(j * LANES, (j + 1) * LANES)
            block[:, lanes] = ef[pl.ds(place(j), NZ, stride=PAD), :].astype(jnp.bfloat16)

        def features(x_of):
            return pl.ds(pl.multiple_of(first_chunk(x_of) * LANES, LANES), KW)

        for k in range(1, NX):
            to = lax.rem(x + k, NX)
            send(block.at[:, features(to)], part.at[x], KS, KR, at(to, z, pipe))

        for q, lanes in SHARES.items():

            @pl.when(pipe == q)
            def _(lanes=lanes):
                for k in range(1, NX):
                    to = at(lax.rem(x + k, NX), z, 1)
                    send(block.at[:, lanes], full.at[x, :, lanes], FS, FR, to)

        @pl.when(lead)
        def _():
            full[x] = block[...]

        part[x] = block[:, features(x)]
        wait_for(part.at[0:3], KR)
        scaled = part[...].reshape(NX * NZ, KW).astype(jnp.float32) * gl[:, features(x)]
        product = jnp.dot(
            scaled.astype(jnp.bfloat16), wk[...], preferred_element_type=jnp.float32
        )
        slot = y * NX + x
        kp[slot] = product.astype(jnp.bfloat16)
        for k in range(NX):
            to = lax.rem(x + k, NX)

            def share(to=to):
                send(kp.at[slot], kp.at[slot], PS, PR, at(to, z, 1))

            if k:
                share()
            else:
                pl.when(jnp.logical_not(lead))(share)

    @pl.when(lead)
    def _():
        wait_for(full.at[0:3], FR)
        out = pltpu.make_async_copy(full, table_out, sem.at[O2])
        out.start()
        squares = jnp.zeros((NX * NZ, LANES), jnp.float32)
        for j in range(NCH):
            wide = full[:, :, LANES * j : LANES * (j + 1)].astype(jnp.float32)
            wide = wide.reshape(NX * NZ, LANES)
            squares = squares + wide * wide
        scale = lax.rsqrt(jnp.sum(squares, axis=-1, keepdims=True) / D + 1e-06)
        wait_for(kp.at[0 : NX * NP // 2 - 1], PR)
        for s in range(NP // 2):
            raw = kp[s * NX].astype(jnp.float32)
            for k in range(1, NX):
                raw = raw + kp[s * NX + k].astype(jnp.float32)
            raw = raw * scale
            for h in range(2):
                head = raw[:, h * HEAD_DIM : (h + 1) * HEAD_DIM]
                mean = jnp.mean(head * head, axis=-1, keepdims=True)
                first = s * HEADS2 + h * HEAD_DIM
                keys[:, first : first + HEAD_DIM] = (
                    head * lax.rsqrt(mean + 1e-06) * kg[...]
                ).astype(jnp.bfloat16)
        last_out = pltpu.make_async_copy(keys, keys_out, sem.at[O3])
        last_out.start()
        out.wait()
        last_out.wait()

    keep.wait()

    @pl.when(pipe == 0)
    def _():
        wait_for(gx, XS)

    @pl.when(last)
    def _():
        wait_for(gx.at[0 : NX - 1], XS)

    @pl.when(reducer)
    def _():
        wait_for(ezr.at[0 : NZ - 1], ZS)
        for q in range(NP - 1):
            wait_for(yr.at[0], YS)

    @pl.when(jnp.logical_not(worker))
    def _():
        wait_for(hz, WAS)
        wait_for(hz.at[0 : NZ - 1], WAS)

    @pl.when(worker)
    def _():
        wait_for(wc, W0S)
        wait_for(ezr.at[0 : NZ - 1], ES)
        wait_for(part.at[0:3], KS)
        wait_for(kp.at[0:3], PS)

        for q, lanes in SHARES.items():

            @pl.when(pipe == q)
            def _(lanes=lanes):
                wait_for(full.at[0 : NX - 1, :, lanes], FS)

        @pl.when(jnp.logical_not(lead))
        def _():
            wait_for(kp.at[0], PS)


PARTS = 6


def look_up_kernel(
    table, keys, step, tokens,
    master_out, one_out, two_out, section_input, section_keys,
    table_v, keys_v, step_v, tokens_v, rows_v, looked, looked_keys, sem,
):
    lead = lax.axis_index("pipe") == 1
    width = D // PARTS

    def move(src, dst, which):
        copy = pltpu.make_async_copy(src, dst, sem.at[which])
        copy.start()
        return copy

    def give(part):
        lanes = slice(part * width, (part + 1) * width)
        return move(looked.at[:, lanes], section_input.at[:, lanes], part)

    load_step = move(step, step_v, 6)

    def finish(gives):
        load_step.wait()
        for j in range(NCH):
            lanes = slice(j * LANES, (j + 1) * LANES)
            for k in range(3):
                rows_v[k, :, lanes] = step_v[k, place(j) : place(j) + 1, :]
        for k, out in enumerate((master_out, one_out, two_out)):
            gives.append(move(rows_v.at[k], out, 11 + k))
        for copy in gives:
            copy.wait()

    @pl.when(lead)
    def _():
        load_tokens = move(tokens, tokens_v, 7)
        loads = []
        for part in range(PARTS):
            lanes = slice(part * width, (part + 1) * width)
            loads.append(move(table.at[:, :, lanes], table_v.at[:, :, lanes], 14 + part))
        load_keys = move(keys, keys_v, 9)
        load_tokens.wait()
        rows = lax.broadcasted_iota(jnp.int32, (NX * NZ, tokens_v.shape[1]), 0)
        hot = jnp.where(rows == tokens_v[...], 1.0, 0.0).T.astype(jnp.bfloat16)
        gives = []
        for part in range(PARTS):
            lanes = slice(part * width, (part + 1) * width)
            loads[part].wait()
            columns = table_v[:, :, lanes].reshape(NX * NZ, width)
            looked[:, lanes] = jnp.dot(
                hot, columns, preferred_element_type=jnp.float32
            ).astype(jnp.bfloat16)
            gives.append(give(part))
        load_keys.wait()
        looked_keys[...] = jnp.dot(
            hot, keys_v[...], preferred_element_type=jnp.float32
        ).astype(jnp.bfloat16)
        gives.append(move(looked_keys, section_keys, 10))
        finish(gives)

    @pl.when(jnp.logical_not(lead))
    def _():
        looked[...] = jnp.zeros_like(looked)
        looked_keys[...] = jnp.zeros_like(looked_keys)
        gives = [give(part) for part in range(PARTS)]
        gives.append(move(looked_keys, section_keys, 10))
        finish(gives)


def shards(
    grad_partials, master, moment_one, moment_two, token_rows, input_gain, key_weight, key_gain
):
    rows, kvw, count = NX * NZ, NP * HEAD_DIM, token_rows.shape[0]
    bf16, f32 = jnp.bfloat16, jnp.float32
    hbm = pl.BlockSpec(memory_space=pl.ANY)
    table, keys, step = pl.pallas_call(
        comm_kernel,
        out_shape=(
            jax.ShapeDtypeStruct((NX, NZ, D), bf16),
            jax.ShapeDtypeStruct((rows, kvw), bf16),
            jax.ShapeDtypeStruct((3, PAD, LANES), f32),
        ),
        in_specs=[hbm] * 7,
        out_specs=(hbm,) * 3,
        scratch_shapes=[
            pltpu.VMEM((NX, NZ, D), bf16),
            pltpu.VMEM((NZ * PAD, LANES), f32),
            pltpu.VMEM((NZ, PAD, LANES), bf16),
            pltpu.VMEM((2 * REACH, PAD, LANES), bf16),
            pltpu.VMEM((REACH, PAD, LANES), bf16),
            pltpu.VMEM((REACH - 1, PAD, LANES), bf16),
            pltpu.VMEM((2, PAD, LANES), bf16),
            pltpu.VMEM((2, PAD, LANES), f32),
            pltpu.VMEM((3, 1, D), f32),
            pltpu.VMEM((3, PAD, LANES), f32),
            pltpu.VMEM((PAD, LANES), bf16),
            pltpu.VMEM((NZ, PAD, LANES), bf16),
            pltpu.VMEM((NZ * PAD, LANES), f32),
            pltpu.VMEM((NZ, D), bf16),
            pltpu.VMEM((NX, NZ, D), bf16),
            pltpu.VMEM((NX, NZ, KW), bf16),
            pltpu.VMEM((WROWS, LANES), bf16),
            pltpu.VMEM((WPAD, LANES), bf16),
            pltpu.VMEM((WPAD, HEADS2), bf16),
            pltpu.VMEM((NZ, WPAD, HEADS2), bf16),
            pltpu.VMEM((4, 4, WPAD, HEADS2), bf16),
            pltpu.VMEM((WPAD, LANES), f32),
            pltpu.VMEM((KW, HEADS2), bf16),
            pltpu.VMEM((NX * NP // 2, rows, HEADS2), bf16),
            pltpu.VMEM((NCH, LANES), f32),
            pltpu.VMEM((1, D), f32),
            pltpu.VMEM((1, HEAD_DIM), f32),
            pltpu.VMEM((3, PAD, LANES), f32),
            pltpu.VMEM((rows, kvw), bf16),
            pltpu.SemaphoreType.DMA((SEMS,)),
        ],
        compiler_params=pltpu.CompilerParams(
            collective_id=0, has_side_effects=True, vmem_limit_bytes=VMEM_BYTES
        ),
        name="sum_step_gather",
    )(
        grad_partials, master, moment_one, moment_two, key_weight,
        input_gain.reshape(NCH, LANES), key_gain.reshape(1, HEAD_DIM),
    )
    line = jax.ShapeDtypeStruct((1, D), f32)
    new_master, new_one, new_two, section_input, section_keys = pl.pallas_call(
        look_up_kernel,
        out_shape=(
            line, line, line,
            jax.ShapeDtypeStruct((count, D), bf16),
            jax.ShapeDtypeStruct((count, kvw), bf16),
        ),
        in_specs=[hbm] * 4,
        out_specs=(hbm,) * 5,
        scratch_shapes=[
            pltpu.VMEM((NX, NZ, D), bf16),
            pltpu.VMEM((rows, kvw), bf16),
            pltpu.VMEM((3, PAD, LANES), f32),
            pltpu.VMEM((1, count), jnp.int32),
            pltpu.VMEM((3, 1, D), f32),
            pltpu.VMEM((count, D), bf16),
            pltpu.VMEM((count, kvw), bf16),
            pltpu.SemaphoreType.DMA((14 + PARTS,)),
        ],
        compiler_params=pltpu.CompilerParams(vmem_limit_bytes=VMEM_BYTES),
        name="look_up",
    )(table, keys, step, token_rows.reshape(1, count))
    return new_master, new_one, new_two, section_input[None], section_keys[None]


def solution(mesh):
    in_specs = (
        P("pipe", "dp", None, None),
        P("dp", None),
        P("dp", None),
        P("dp", None),
        P("dp"),
        P(),
        P("dp", "pipe"),
        P(),
    )
    out_specs = (
        P("dp", None),
        P("dp", None),
        P("dp", None),
        P("pipe", "dp", None),
        P("pipe", "dp", None),
    )
    return jax.shard_map(shards, mesh=mesh, in_specs=in_specs, out_specs=out_specs, check_vma=False)
```

```python
import jax
import jax.numpy as jnp
from jax import lax
from jax.experimental import pallas as pl
from jax.experimental.pallas import tpu as pltpu
from jax.sharding import PartitionSpec as P

MESH = pl.DeviceIdType.MESH
HEAD_DIM = 128
LANES = 128
NX, NZ, NP = 4, 16, 8
D = 5376
NCH = D // LANES
PAD = 48
WROWS = 84
WPAD = 96
KC = 11
KW = KC * LANES
HEADS2 = 2 * HEAD_DIM
VMEM_BYTES = 60 * 2**20
SHARES = {1: slice(0, 2688), 3: slice(2688, 4096), 7: slice(4096, D)}

(
    XS, ZS, YS, YR0, YR1, W0S, W0R, WAS, WB,
    ES, EM, EP, ER, KS, KR, FS, FR, PS, PR, LM, L1, L2, LW, LG, LK, O1, O2, O3, XR,
) = range(29)
THIRDS, BAND = 3, 14
ZR, RP, RM, WR = XR + THIRDS, XR + 2 * THIRDS, XR + 3 * THIRDS, XR + 4 * THIRDS
SEMS = WR + NZ
REACH = 4


def place(j):
    return j // BAND * 16 + j % BAND


def first_chunk(x):
    return (x // 2) * 21 + lax.rem(x, 2) * 10


def comm_kernel(
    grad, master, moment_one, moment_two, weight, gain, key_gain,
    table_out, keys_out, step_out,
    gx, zs, zb, zr, zp, zm, zq, yr, state, prior, erow, ezr, ef, block, full, part, wv, wc, wp, hz, wz, wf, wk, kp,
    gv, gl, kg, step, keys, sem,
):
    dp = lax.axis_index("dp")
    pipe = lax.axis_index("pipe")
    x, z = dp // NZ, lax.rem(dp, NZ)
    y = pipe // 2
    worker = lax.rem(pipe, 2) == 1
    mate = jnp.where(worker, pipe - 1, pipe + 1)
    lead, last = pipe == 1, pipe == NP - 1
    reducer = jnp.logical_or(lead, last)

    def at(x_to, z_to, pipe_to):
        return (x_to * NZ + z_to, pipe_to)

    def send(src, dst, sent, arrived, where):
        pltpu.make_async_remote_copy(
            src_ref=src, dst_ref=dst, send_sem=sem.at[sent], recv_sem=sem.at[arrived],
            device_id=where, device_id_type=MESH,
        ).start()

    def wait_for(like, which):
        pltpu.make_async_copy(like, like, sem.at[which]).wait()

    barrier = pltpu.get_barrier_semaphore()

    def tell(where):
        pl.semaphore_signal(barrier, inc=1, device_id=where, device_id_type=MESH)

    def away(k):
        return lax.rem(z + k + NZ, NZ)

    near = [k for k in range(-REACH, REACH + 1) if k]

    @pl.when(worker)
    def _():
        for k in near:
            tell(at(x, away(k), pipe))
        for k in range(1, NX):
            tell(at(lax.rem(x + k, NX), z, pipe))
        tell((dp, mate))

    @pl.when(lead)
    def _():
        for k in range(1, NX):
            tell(at(lax.rem(x + k, NX), z, 0))

    @pl.when(jnp.logical_not(worker))
    def _():
        for k in (1, -1, 2, -2):
            tell(at(x, away(k), pipe))

    @pl.when(jnp.logical_or(pipe == 2, pipe == 4))
    def _():
        tell((dp, mate))

    @pl.when(jnp.logical_not(lead))
    def _():
        tell((dp, 1))

    @pl.when(jnp.logical_not(last))
    def _():
        tell((dp, NP - 1))

    @pl.when(lead)
    def _():
        for k in range(NX):
            for q in (3, 5, 7):
                if k > 0 or q != 7:
                    tell(at(lax.rem(x + k, NX), z, q))

    def load(src, dst, which):
        copy = pltpu.make_async_copy(src, dst, sem.at[which])
        copy.start()
        return copy

    load_weight = load(weight, wv, LW)
    load_state = [
        load(master, state.at[0], LM), load(moment_one, state.at[1], L1),
        load(moment_two, state.at[2], L2),
    ]
    load_gain = load(gain, gv, LG)
    load_key_gain = load(key_gain, kg, LK)

    peers = len(near) + NX - 1
    counts = {
        0: 5 + NX - 1, 2: 5, 4: 5, 6: 5,
        1: peers + NP - 1, 7: peers + NP - 1 + NX - 1, 3: peers + NX + 1, 5: peers + NX + 1,
    }
    for q, count in counts.items():

        @pl.when(pipe == q)
        def _(count=count):
            pl.semaphore_wait(barrier, count)

    for here in (0, NP - 1):

        @pl.when(pipe == here)
        def _(here=here):
            for band in range(THIRDS):
                lanes = slice(band * BAND * LANES, (band + 1) * BAND * LANES)
                for k in (2, 1, 3, 0):
                    to = lax.rem(x + k, NX)
                    rows = pl.ds(pl.multiple_of(to * NZ, NZ), NZ)
                    src, dst = grad.at[0, 0, rows, lanes], gx.at[x, :, lanes]
                    if here and not k:
                        load(src, dst, XR + band)
                    else:
                        send(src, dst, XS, XR + band, at(to, z, 1 if here == 0 else here))

    load_weight.wait()
    wc[...] = jnp.zeros_like(wc)
    wide = wv[...].astype(jnp.float32)
    for q in range(4):
        @pl.when(lax.rem(z, 4) == q)
        def _(q=q):
            wf[...] = jnp.zeros_like(wf)
            wf[4 * q : 4 * q + WROWS, :] = wide
            wc[...] = wf[...].astype(jnp.bfloat16)

    @pl.when(worker)
    def _():
        send(wc, wp.at[:, LANES:HEADS2], W0S, W0R, (dp, mate))

    @pl.when(jnp.logical_not(worker))
    def _():
        wp[:, 0:LANES] = wc[...]

    def weights_on(way, step):
        row, first, limit = away(-way * step), (WR if way > 0 else WR + 8), (8 if way > 0 else 7)
        if step % 2 == 0:
            for k in (2, 1):
                if step + k <= limit:
                    to = at(x, away(way * k), pipe)
                    send(hz.at[row], hz.at[row], WAS, first + step + k - 1, to)

    def weights_in(way, step):
        wait_for(wp, (WR if way > 0 else WR + 8) + step - 1)
        weights_on(way, step)
        row = away(-way * step)
        send(hz.at[row], wz.at[lax.rem(row, 4), row // 4], WAS, WB, (dp, mate))

    @pl.when(jnp.logical_not(worker))
    def _():
        wait_for(wc, W0R)
        hz[z] = wp[...]
        weights_on(1, 0)
        weights_on(-1, 0)
        send(hz.at[z], wz.at[lax.rem(z, 4), z // 4], WAS, WB, (dp, mate))
        for step in (2, 1, 4, 3, 6, 5, 8, 7):
            weights_in(1, step)
            if step < 8:
                weights_in(-1, step)

    prior[...] = jnp.zeros_like(prior)
    for copy in load_state:
        copy.wait()
    for j in range(NCH):
        lanes = slice(j * LANES, (j + 1) * LANES)
        for k in range(3):
            prior[k, place(j) : place(j) + 1, :] = state[k, :, lanes]

    load_gain.wait()
    load_key_gain.wait()

    def weights_join():
        wait_for(wz, WB)
        side = lax.rem(x, 2)
        spare = pl.multiple_of((1 - side) * NZ * WROWS, 64)
        wk[pl.ds(spare, 64), :] = jnp.zeros((64, HEADS2), jnp.bfloat16)
        for g in range(4):
            start = pl.multiple_of(side * 64 + g * 4 * WROWS, 16)

            def put(row, value):
                wk[pl.ds(pl.multiple_of(start + row, 16), value.shape[0]), :] = value

            for k in range(4):
                edge = wz[k, g, 0:16, :]
                if k:
                    edge = edge + wz[k - 1, g, 80:96, :]
                put(80 * k, edge)
                put(80 * k + 16, wz[k, g, 16:80, :])
            put(320, wz[3, g, 80:96, :])
        for j in range(NCH):
            gl[:, j * LANES : (j + 1) * LANES] = gv[j : j + 1, :]

    def row_sum(refs):
        total = refs[0].astype(jnp.float32)
        for ref in refs[1:]:
            total = total + ref.astype(jnp.float32)
        return total

    @pl.when(reducer)
    def _():
        zs[...] = jnp.zeros_like(zs)
        for band in range(THIRDS):
            wait_for(gx.at[:, :, 0 : BAND * LANES], XR + band)
            for j in range(band * BAND, (band + 1) * BAND):
                lanes = slice(j * LANES, (j + 1) * LANES)
                total = row_sum([gx[k, :, lanes] for k in range(NX)])
                zs[pl.ds(place(j), NZ, stride=PAD), :] = total
            part_rows = slice(16 * band, 16 * (band + 1))
            for k in range(NZ):
                zb[k, part_rows, :] = zs[
                    PAD * k + 16 * band : PAD * k + 16 * (band + 1), :
                ].astype(jnp.bfloat16)

            def give(row, dst, arrived, k, part_rows=part_rows, band=band):
                send(
                    zb.at[row, part_rows], dst.at[part_rows], ZS, arrived + band,
                    at(x, away(k), pipe),
                )

            for k in range(REACH, 0, -1):
                give(away(k + REACH), zp.at[k - 1], RP, k)
                if k < REACH:
                    give(away(-k - REACH), zm.at[k - 1], RM, -k)
            for k in range(1, REACH):
                give(away(k), zr.at[REACH - k], ZR, k)
                give(away(-k), zr.at[REACH + k - 1], ZR, -k)

        for band in range(THIRDS):
            part_rows = slice(16 * band, 16 * (band + 1))
            ways = (
                (zp, RP, REACH, 0, 0),
                (zm, RM, REACH - 1, 1, 2 * REACH - 1),
            )
            for ref, arrived, count, slot, there in ways:
                k = REACH if slot == 0 else -REACH
                wait_for(ref.at[0:count, part_rows], arrived + band)
                own = zs[pl.ds(pl.multiple_of(away(k) * PAD + 16 * band, 16), 16), :]
                passed = own + row_sum([ref[q, part_rows, :] for q in range(count)])
                zq[slot, part_rows, :] = passed.astype(jnp.bfloat16)
                send(
                    zq.at[slot, part_rows], zr.at[there, part_rows], ZS, ZR + band,
                    at(x, away(k), pipe),
                )

        for band in range(THIRDS):
            wait_for(zr.at[:, 0:16], ZR + band)
        own = zs[pl.ds(pl.multiple_of(z * PAD, PAD), PAD), :]
        total = own + row_sum([zr[k] for k in range(2 * REACH)])

        @pl.when(lead)
        def _():
            yr[0] = total
            for q in (3, 5, 7, 0, 2, 4, 6):
                send(yr.at[0], yr.at[0], YS, YR0, (dp, q))

        @pl.when(last)
        def _():
            yr[1] = total
            for q in (1, 3, 5, 0, 2, 4, 6):
                send(yr.at[1], yr.at[1], YS, YR1, (dp, q))

    @pl.when(jnp.logical_not(lead))
    def _():
        wait_for(yr.at[0], YR0)

    @pl.when(jnp.logical_not(last))
    def _():
        wait_for(yr.at[1], YR1)

    gradient = yr[0] + yr[1]
    new_one = 0.9 * prior[1] + 0.1 * gradient
    new_two = 0.95 * prior[2] + 0.05 * gradient * gradient
    correct_one = 1.0 - 0.9**10
    correct_two = 1.0 - 0.95**10
    update = new_one / correct_one / (jnp.sqrt(new_two / correct_two) + 1e-08)
    new_master = prior[0] - 0.001 * update
    step[0] = new_master
    step[1] = new_one
    step[2] = new_two
    keep = pltpu.make_async_copy(step, step_out, sem.at[O1])

    @pl.when(worker)
    def _():
        table = new_master.astype(jnp.bfloat16).astype(jnp.float32)
        erow[...] = (table * jnp.float32(D**0.5)).astype(jnp.bfloat16)
        for k in (4, -4, 3, -3, 2, -2, 1, -1):
            arrives = {REACH: EM, -REACH: EP}.get(k, ER)
            send(erow, ezr.at[z], ES, arrives, at(x, away(k), pipe))
        ezr[z] = erow[...]

    keep.start()

    @pl.when(worker)
    def _():
        def pass_up():
            wait_for(erow, EM)
            row = away(-REACH)
            for k in range(REACH, 0, -1):
                send(ezr.at[row], ezr.at[row], ES, ER, at(x, away(k), pipe))

        def pass_down():
            wait_for(erow, EP)
            row = away(REACH)
            for k in range(REACH - 1, 0, -1):
                send(ezr.at[row], ezr.at[row], ES, ER, at(x, away(-k), pipe))

        @pl.when(z < NZ // 2)
        def _():
            pass_down()
            pass_up()

        @pl.when(z >= NZ // 2)
        def _():
            pass_up()
            pass_down()

        weights_join()

        wait_for(ezr.at[0 : NZ - 3], ER)
        ef[...] = ezr[...].astype(jnp.float32).reshape(NZ * PAD, LANES)

        for j in range(NCH):
            lanes = slice(j * LANES, (j + 1) * LANES)
            block[:, lanes] = ef[pl.ds(place(j), NZ, stride=PAD), :].astype(jnp.bfloat16)

        def features(x_of):
            return pl.ds(pl.multiple_of(first_chunk(x_of) * LANES, LANES), KW)

        for k in range(1, NX):
            to = lax.rem(x + k, NX)
            send(block.at[:, features(to)], part.at[x], KS, KR, at(to, z, pipe))

        for q, lanes in SHARES.items():

            @pl.when(pipe == q)
            def _(lanes=lanes):
                for k in range(1, NX):
                    to = at(lax.rem(x + k, NX), z, 1)
                    send(block.at[:, lanes], full.at[x, :, lanes], FS, FR, to)

        @pl.when(lead)
        def _():
            full[x] = block[...]

        part[x] = block[:, features(x)]
        wait_for(part.at[0:3], KR)
        scaled = part[...].reshape(NX * NZ, KW).astype(jnp.float32) * gl[:, features(x)]
        product = jnp.dot(
            scaled.astype(jnp.bfloat16), wk[...], preferred_element_type=jnp.float32
        )
        slot = y * NX + x
        kp[slot] = product.astype(jnp.bfloat16)
        for k in (2, 1, 3, 0):
            to = lax.rem(x + k, NX)

            def share(to=to):
                send(kp.at[slot], kp.at[slot], PS, PR, at(to, z, 1))

            if k:
                share()
            else:
                pl.when(jnp.logical_not(lead))(share)

    @pl.when(lead)
    def _():
        wait_for(full.at[0:3], FR)
        out = pltpu.make_async_copy(full, table_out, sem.at[O2])
        out.start()
        squares = jnp.zeros((NX * NZ, LANES), jnp.float32)
        for j in range(NCH):
            wide = full[:, :, LANES * j : LANES * (j + 1)].astype(jnp.float32)
            wide = wide.reshape(NX * NZ, LANES)
            squares = squares + wide * wide
        scale = lax.rsqrt(jnp.sum(squares, axis=-1, keepdims=True) / D + 1e-06)
        wait_for(kp.at[0 : NX * NP // 2 - 1], PR)
        for s in range(NP // 2):
            raw = kp[s * NX].astype(jnp.float32)
            for k in range(1, NX):
                raw = raw + kp[s * NX + k].astype(jnp.float32)
            raw = raw * scale
            for h in range(2):
                head = raw[:, h * HEAD_DIM : (h + 1) * HEAD_DIM]
                mean = jnp.mean(head * head, axis=-1, keepdims=True)
                first = s * HEADS2 + h * HEAD_DIM
                keys[:, first : first + HEAD_DIM] = (
                    head * lax.rsqrt(mean + 1e-06) * kg[...]
                ).astype(jnp.bfloat16)
        last_out = pltpu.make_async_copy(keys, keys_out, sem.at[O3])
        last_out.start()
        out.wait()
        last_out.wait()

    keep.wait()

    @pl.when(pipe == 0)
    def _():
        wait_for(gx, XS)

    @pl.when(last)
    def _():
        wait_for(gx.at[0 : NX - 1], XS)

    @pl.when(reducer)
    def _():
        wait_for(ezr.at[0 : NZ - 1], ZS)
        for q in range(NP - 1):
            wait_for(yr.at[0], YS)

    @pl.when(jnp.logical_not(worker))
    def _():
        wait_for(hz, WAS)
        wait_for(hz.at[0 : NZ - 1], WAS)

    @pl.when(worker)
    def _():
        wait_for(wc, W0S)
        wait_for(ezr.at[0 : NZ - 1], ES)
        wait_for(part.at[0:3], KS)
        wait_for(kp.at[0:3], PS)

        for q, lanes in SHARES.items():

            @pl.when(pipe == q)
            def _(lanes=lanes):
                wait_for(full.at[0 : NX - 1, :, lanes], FS)

        @pl.when(jnp.logical_not(lead))
        def _():
            wait_for(kp.at[0], PS)


PARTS, TOKENS_AT_ONCE = 3, 64


def look_up_kernel(
    table, keys, step, tokens,
    master_out, one_out, two_out, section_input, section_keys,
    table_v, keys_v, step_v, tokens_v, rows_v, looked, looked_keys, sem,
):
    lead = lax.axis_index("pipe") == 1
    width = D // PARTS

    def move(src, dst, which):
        copy = pltpu.make_async_copy(src, dst, sem.at[which])
        copy.start()
        return copy

    def give(first):
        rows = slice(first, first + TOKENS_AT_ONCE)
        return move(looked.at[rows], section_input.at[rows], first // TOKENS_AT_ONCE)

    load_step = move(step, step_v, 6)

    def finish(gives):
        load_step.wait()
        for j in range(NCH):
            lanes = slice(j * LANES, (j + 1) * LANES)
            for k in range(3):
                rows_v[k, :, lanes] = step_v[k, place(j) : place(j) + 1, :]
        for k, out in enumerate((master_out, one_out, two_out)):
            gives.append(move(rows_v.at[k], out, 11 + k))
        for copy in gives:
            copy.wait()

    @pl.when(lead)
    def _():
        load_tokens = move(tokens, tokens_v, 7)
        loads = []
        for part in range(PARTS):
            lanes = slice(part * width, (part + 1) * width)
            loads.append(move(table.at[:, :, lanes], table_v.at[:, :, lanes], 14 + part))
        load_keys = move(keys, keys_v, 9)
        load_tokens.wait()
        rows = lax.broadcasted_iota(jnp.int32, (NX * NZ, tokens_v.shape[1]), 0)
        hot = jnp.where(rows == tokens_v[...], 1.0, 0.0).T.astype(jnp.bfloat16)
        gives = []
        for copy in loads:
            copy.wait()
        for first in range(0, looked.shape[0], TOKENS_AT_ONCE):
            tokens_now = slice(first, first + TOKENS_AT_ONCE)
            for part in range(PARTS):
                lanes = slice(part * width, (part + 1) * width)
                looked[tokens_now, lanes] = jnp.dot(
                    hot[tokens_now], table_v[:, :, lanes].reshape(NX * NZ, width),
                    preferred_element_type=jnp.float32,
                ).astype(jnp.bfloat16)
            gives.append(give(first))
        load_keys.wait()
        looked_keys[...] = jnp.dot(
            hot, keys_v[...], preferred_element_type=jnp.float32
        ).astype(jnp.bfloat16)
        gives.append(move(looked_keys, section_keys, 10))
        finish(gives)

    @pl.when(jnp.logical_not(lead))
    def _():
        looked[...] = jnp.zeros_like(looked)
        looked_keys[...] = jnp.zeros_like(looked_keys)
        gives = [give(first) for first in range(0, looked.shape[0], TOKENS_AT_ONCE)]
        gives.append(move(looked_keys, section_keys, 10))
        finish(gives)


def shards(
    grad_partials, master, moment_one, moment_two, token_rows, input_gain, key_weight, key_gain
):
    rows, kvw, count = NX * NZ, NP * HEAD_DIM, token_rows.shape[0]
    bf16, f32 = jnp.bfloat16, jnp.float32
    hbm = pl.BlockSpec(memory_space=pl.ANY)
    table, keys, step = pl.pallas_call(
        comm_kernel,
        out_shape=(
            jax.ShapeDtypeStruct((NX, NZ, D), bf16),
            jax.ShapeDtypeStruct((rows, kvw), bf16),
            jax.ShapeDtypeStruct((3, PAD, LANES), f32),
        ),
        in_specs=[hbm] * 7,
        out_specs=(hbm,) * 3,
        scratch_shapes=[
            pltpu.VMEM((NX, NZ, D), bf16),
            pltpu.VMEM((NZ * PAD, LANES), f32),
            pltpu.VMEM((NZ, PAD, LANES), bf16),
            pltpu.VMEM((2 * REACH, PAD, LANES), bf16),
            pltpu.VMEM((REACH, PAD, LANES), bf16),
            pltpu.VMEM((REACH - 1, PAD, LANES), bf16),
            pltpu.VMEM((2, PAD, LANES), bf16),
            pltpu.VMEM((2, PAD, LANES), f32),
            pltpu.VMEM((3, 1, D), f32),
            pltpu.VMEM((3, PAD, LANES), f32),
            pltpu.VMEM((PAD, LANES), bf16),
            pltpu.VMEM((NZ, PAD, LANES), bf16),
            pltpu.VMEM((NZ * PAD, LANES), f32),
            pltpu.VMEM((NZ, D), bf16),
            pltpu.VMEM((NX, NZ, D), bf16),
            pltpu.VMEM((NX, NZ, KW), bf16),
            pltpu.VMEM((WROWS, LANES), bf16),
            pltpu.VMEM((WPAD, LANES), bf16),
            pltpu.VMEM((WPAD, HEADS2), bf16),
            pltpu.VMEM((NZ, WPAD, HEADS2), bf16),
            pltpu.VMEM((4, 4, WPAD, HEADS2), bf16),
            pltpu.VMEM((WPAD, LANES), f32),
            pltpu.VMEM((KW, HEADS2), bf16),
            pltpu.VMEM((NX * NP // 2, rows, HEADS2), bf16),
            pltpu.VMEM((NCH, LANES), f32),
            pltpu.VMEM((1, D), f32),
            pltpu.VMEM((1, HEAD_DIM), f32),
            pltpu.VMEM((3, PAD, LANES), f32),
            pltpu.VMEM((rows, kvw), bf16),
            pltpu.SemaphoreType.DMA((SEMS,)),
        ],
        compiler_params=pltpu.CompilerParams(
            collective_id=0, has_side_effects=True, vmem_limit_bytes=VMEM_BYTES
        ),
        name="sum_step_gather",
    )(
        grad_partials, master, moment_one, moment_two, key_weight,
        input_gain.reshape(NCH, LANES), key_gain.reshape(1, HEAD_DIM),
    )
    line = jax.ShapeDtypeStruct((1, D), f32)
    new_master, new_one, new_two, section_input, section_keys = pl.pallas_call(
        look_up_kernel,
        out_shape=(
            line, line, line,
            jax.ShapeDtypeStruct((count, D), bf16),
            jax.ShapeDtypeStruct((count, kvw), bf16),
        ),
        in_specs=[hbm] * 4,
        out_specs=(hbm,) * 5,
        scratch_shapes=[
            pltpu.VMEM((NX, NZ, D), bf16),
            pltpu.VMEM((rows, kvw), bf16),
            pltpu.VMEM((3, PAD, LANES), f32),
            pltpu.VMEM((1, count), jnp.int32),
            pltpu.VMEM((3, 1, D), f32),
            pltpu.VMEM((count, D), bf16),
            pltpu.VMEM((count, kvw), bf16),
            pltpu.SemaphoreType.DMA((14 + PARTS,)),
        ],
        compiler_params=pltpu.CompilerParams(vmem_limit_bytes=VMEM_BYTES),
        name="look_up",
    )(table, keys, step, token_rows.reshape(1, count))
    return new_master, new_one, new_two, section_input[None], section_keys[None]


def solution(mesh):
    in_specs = (
        P("pipe", "dp", None, None),
        P("dp", None),
        P("dp", None),
        P("dp", None),
        P("dp"),
        P(),
        P("dp", "pipe"),
        P(),
    )
    out_specs = (
        P("dp", None),
        P("dp", None),
        P("dp", None),
        P("pipe", "dp", None),
        P("pipe", "dp", None),
    )
    return jax.shard_map(shards, mesh=mesh, in_specs=in_specs, out_specs=out_specs, check_vma=False)
```

```python
import jax
import jax.numpy as jnp
from jax import lax
from jax.experimental import pallas as pl
from jax.experimental.pallas import tpu as pltpu
from jax.sharding import PartitionSpec as P

MESH = pl.DeviceIdType.MESH
HEAD_DIM = 128
LANES = 128
NX, NZ, NP = 4, 16, 8
D = 5376
NCH = D // LANES
PAD = 48
WROWS = 84
WPAD = 96
KC = 11
KW = KC * LANES
HEADS2 = 2 * HEAD_DIM
VMEM_BYTES = 60 * 2**20
SHARES = {1: slice(0, 2688), 3: slice(2688, 4096), 7: slice(4096, D)}

(
    XS, ZS, YS, YR0, YR1, W0S, W0R, WAS, WB,
    ES, EM, EP, ER, KS, KR, FS, FR, PS, PR, LM, L1, L2, LW, LG, LK, O1, O2, O3, XR,
) = range(29)
THIRDS, BAND = 3, 14
ZR, RP, RM, WR = XR + THIRDS, XR + 2 * THIRDS, XR + 3 * THIRDS, XR + 4 * THIRDS
SEMS = WR + NZ
REACH = 4


def place(j):
    return j // BAND * 16 + j % BAND


def first_chunk(x):
    return (x // 2) * 21 + lax.rem(x, 2) * 10


def comm_kernel(
    grad, master, moment_one, moment_two, weight, gain, key_gain,
    table_out, keys_out, step_out,
    gx, zs, zb, zr, zp, zm, zq, yr, state, prior, erow, ezr, ef, block, full, part, wv, wc, wp, hz, wz, wf, wk, kp,
    gv, gl, kg, step, keys, sem,
):
    dp = lax.axis_index("dp")
    pipe = lax.axis_index("pipe")
    x, z = dp // NZ, lax.rem(dp, NZ)
    y = pipe // 2
    worker = lax.rem(pipe, 2) == 1
    mate = jnp.where(worker, pipe - 1, pipe + 1)
    lead, last = pipe == 1, pipe == NP - 1
    reducer = jnp.logical_or(lead, last)

    def at(x_to, z_to, pipe_to):
        return (x_to * NZ + z_to, pipe_to)

    def send(src, dst, sent, arrived, where):
        pltpu.make_async_remote_copy(
            src_ref=src, dst_ref=dst, send_sem=sem.at[sent], recv_sem=sem.at[arrived],
            device_id=where, device_id_type=MESH,
        ).start()

    def wait_for(like, which):
        pltpu.make_async_copy(like, like, sem.at[which]).wait()

    barrier = pltpu.get_barrier_semaphore()

    def tell(where):
        pl.semaphore_signal(barrier, inc=1, device_id=where, device_id_type=MESH)

    def away(k):
        return lax.rem(z + k + NZ, NZ)

    near = [k for k in range(-REACH, REACH + 1) if k]

    @pl.when(worker)
    def _():
        for k in near:
            tell(at(x, away(k), pipe))
        for k in range(1, NX):
            tell(at(lax.rem(x + k, NX), z, pipe))
        tell((dp, mate))

    @pl.when(lead)
    def _():
        for k in range(1, NX):
            tell(at(lax.rem(x + k, NX), z, 0))

    @pl.when(jnp.logical_not(worker))
    def _():
        for k in (1, -1, 2, -2):
            tell(at(x, away(k), pipe))

    @pl.when(jnp.logical_or(pipe == 2, pipe == 4))
    def _():
        tell((dp, mate))

    @pl.when(jnp.logical_not(lead))
    def _():
        tell((dp, 1))

    @pl.when(jnp.logical_not(last))
    def _():
        tell((dp, NP - 1))

    @pl.when(lead)
    def _():
        for k in range(NX):
            for q in (3, 5, 7):
                if k > 0 or q != 7:
                    tell(at(lax.rem(x + k, NX), z, q))

    def load(src, dst, which):
        copy = pltpu.make_async_copy(src, dst, sem.at[which])
        copy.start()
        return copy

    load_weight = load(weight, wv, LW)
    load_state = [
        load(master, state.at[0], LM), load(moment_one, state.at[1], L1),
        load(moment_two, state.at[2], L2),
    ]
    load_gain = load(gain, gv, LG)
    load_key_gain = load(key_gain, kg, LK)

    peers = len(near) + NX - 1
    counts = {
        0: 5 + NX - 1, 2: 5, 4: 5, 6: 5,
        1: peers + NP - 1, 7: peers + NP - 1 + NX - 1, 3: peers + NX + 1, 5: peers + NX + 1,
    }
    for q, count in counts.items():

        @pl.when(pipe == q)
        def _(count=count):
            pl.semaphore_wait(barrier, count)

    for here in (0, NP - 1):

        @pl.when(pipe == here)
        def _(here=here):
            for band in range(THIRDS):
                lanes = slice(band * BAND * LANES, (band + 1) * BAND * LANES)
                for k in (2, 1, 3, 0):
                    to = lax.rem(x + k, NX)
                    rows = pl.ds(pl.multiple_of(to * NZ, NZ), NZ)
                    src, dst = grad.at[0, 0, rows, lanes], gx.at[x, :, lanes]
                    if here and not k:
                        load(src, dst, XR + band)
                    else:
                        send(src, dst, XS, XR + band, at(to, z, 1 if here == 0 else here))

    load_weight.wait()
    wc[...] = jnp.zeros_like(wc)
    wide = wv[...].astype(jnp.float32)
    for q in range(4):
        @pl.when(lax.rem(z, 4) == q)
        def _(q=q):
            wf[...] = jnp.zeros_like(wf)
            wf[4 * q : 4 * q + WROWS, :] = wide
            wc[...] = wf[...].astype(jnp.bfloat16)

    @pl.when(worker)
    def _():
        send(wc, wp.at[:, LANES:HEADS2], W0S, W0R, (dp, mate))

    @pl.when(jnp.logical_not(worker))
    def _():
        wp[:, 0:LANES] = wc[...]

    def weights_on(way, step):
        row, first, limit = away(-way * step), (WR if way > 0 else WR + 8), (8 if way > 0 else 7)
        if step % 2 == 0:
            for k in (2, 1):
                if step + k <= limit:
                    to = at(x, away(way * k), pipe)
                    send(hz.at[row], hz.at[row], WAS, first + step + k - 1, to)

    def weights_in(way, step):
        wait_for(wp, (WR if way > 0 else WR + 8) + step - 1)
        weights_on(way, step)
        row = away(-way * step)
        send(hz.at[row], wz.at[lax.rem(row, 4), row // 4], WAS, WB, (dp, mate))

    @pl.when(jnp.logical_not(worker))
    def _():
        wait_for(wc, W0R)
        hz[z] = wp[...]
        weights_on(1, 0)
        weights_on(-1, 0)
        send(hz.at[z], wz.at[lax.rem(z, 4), z // 4], WAS, WB, (dp, mate))
        for step in (2, 1, 4, 3, 6, 5, 8, 7):
            weights_in(1, step)
            if step < 8:
                weights_in(-1, step)

    prior[...] = jnp.zeros_like(prior)
    for copy in load_state:
        copy.wait()
    for j in range(NCH):
        lanes = slice(j * LANES, (j + 1) * LANES)
        for k in range(3):
            prior[k, place(j) : place(j) + 1, :] = state[k, :, lanes]

    load_gain.wait()
    load_key_gain.wait()

    def weights_join():
        wait_for(wz, WB)
        side = lax.rem(x, 2)
        spare = pl.multiple_of((1 - side) * NZ * WROWS, 64)
        wk[pl.ds(spare, 64), :] = jnp.zeros((64, HEADS2), jnp.bfloat16)
        for g in range(4):
            start = pl.multiple_of(side * 64 + g * 4 * WROWS, 16)

            def put(row, value):
                wk[pl.ds(pl.multiple_of(start + row, 16), value.shape[0]), :] = value

            for k in range(4):
                edge = wz[k, g, 0:16, :]
                if k:
                    edge = edge + wz[k - 1, g, 80:96, :]
                put(80 * k, edge)
                put(80 * k + 16, wz[k, g, 16:80, :])
            put(320, wz[3, g, 80:96, :])
        for j in range(NCH):
            gl[:, j * LANES : (j + 1) * LANES] = gv[j : j + 1, :]

    def row_sum(refs):
        total = refs[0].astype(jnp.float32)
        for ref in refs[1:]:
            total = total + ref.astype(jnp.float32)
        return total

    @pl.when(reducer)
    def _():
        zs[...] = jnp.zeros_like(zs)
        for band in range(THIRDS):
            wait_for(gx.at[:, :, 0 : BAND * LANES], XR + band)
            for j in range(band * BAND, (band + 1) * BAND):
                lanes = slice(j * LANES, (j + 1) * LANES)
                total = row_sum([gx[k, :, lanes] for k in range(NX)])
                zs[pl.ds(place(j), NZ, stride=PAD), :] = total
            part_rows = slice(16 * band, 16 * (band + 1))
            for k in range(NZ):
                zb[k, part_rows, :] = zs[
                    PAD * k + 16 * band : PAD * k + 16 * (band + 1), :
                ].astype(jnp.bfloat16)

            def give(row, dst, arrived, k, part_rows=part_rows, band=band):
                send(
                    zb.at[row, part_rows], dst.at[part_rows], ZS, arrived + band,
                    at(x, away(k), pipe),
                )

            for k in range(REACH, 0, -1):
                give(away(k + REACH), zp.at[k - 1], RP, k)
                if k < REACH:
                    give(away(-k - REACH), zm.at[k - 1], RM, -k)
            for k in range(1, REACH):
                give(away(k), zr.at[REACH - k], ZR, k)
                give(away(-k), zr.at[REACH + k - 1], ZR, -k)

        for band in range(THIRDS):
            part_rows = slice(16 * band, 16 * (band + 1))
            ways = (
                (zp, RP, REACH, 0, 0),
                (zm, RM, REACH - 1, 1, 2 * REACH - 1),
            )
            for ref, arrived, count, slot, there in ways:
                k = REACH if slot == 0 else -REACH
                wait_for(ref.at[0:count, part_rows], arrived + band)
                own = zs[pl.ds(pl.multiple_of(away(k) * PAD + 16 * band, 16), 16), :]
                passed = own + row_sum([ref[q, part_rows, :] for q in range(count)])
                zq[slot, part_rows, :] = passed.astype(jnp.bfloat16)
                send(
                    zq.at[slot, part_rows], zr.at[there, part_rows], ZS, ZR + band,
                    at(x, away(k), pipe),
                )

        for band in range(THIRDS):
            wait_for(zr.at[:, 0:16], ZR + band)
        own = zs[pl.ds(pl.multiple_of(z * PAD, PAD), PAD), :]
        total = own + row_sum([zr[k] for k in range(2 * REACH)])

        @pl.when(lead)
        def _():
            yr[0] = total
            for q in (3, 5, 7, 0, 2, 4, 6):
                send(yr.at[0], yr.at[0], YS, YR0, (dp, q))

        @pl.when(last)
        def _():
            yr[1] = total
            for q in (1, 3, 5, 0, 2, 4, 6):
                send(yr.at[1], yr.at[1], YS, YR1, (dp, q))

    @pl.when(jnp.logical_not(lead))
    def _():
        wait_for(yr.at[0], YR0)

    @pl.when(jnp.logical_not(last))
    def _():
        wait_for(yr.at[1], YR1)

    gradient = yr[0] + yr[1]
    new_one = 0.9 * prior[1] + 0.1 * gradient
    new_two = 0.95 * prior[2] + 0.05 * gradient * gradient
    correct_one = 1.0 - 0.9**10
    correct_two = 1.0 - 0.95**10
    update = new_one / correct_one / (jnp.sqrt(new_two / correct_two) + 1e-08)
    new_master = prior[0] - 0.001 * update
    step[0] = new_master
    step[1] = new_one
    step[2] = new_two
    keep = pltpu.make_async_copy(step, step_out, sem.at[O1])

    @pl.when(worker)
    def _():
        table = new_master.astype(jnp.bfloat16).astype(jnp.float32)
        erow[...] = (table * jnp.float32(D**0.5)).astype(jnp.bfloat16)
        for k in (4, -4, 3, -3, 2, -2, 1, -1):
            arrives = {REACH: EM, -REACH: EP}.get(k, ER)
            send(erow, ezr.at[z], ES, arrives, at(x, away(k), pipe))
        ezr[z] = erow[...]

    keep.start()

    @pl.when(worker)
    def _():
        def pass_up():
            wait_for(erow, EM)
            row = away(-REACH)
            for k in range(REACH, 0, -1):
                send(ezr.at[row], ezr.at[row], ES, ER, at(x, away(k), pipe))

        def pass_down():
            wait_for(erow, EP)
            row = away(REACH)
            for k in range(REACH - 1, 0, -1):
                send(ezr.at[row], ezr.at[row], ES, ER, at(x, away(-k), pipe))

        @pl.when(z < NZ // 2)
        def _():
            pass_down()
            pass_up()

        @pl.when(z >= NZ // 2)
        def _():
            pass_up()
            pass_down()

        weights_join()

        wait_for(ezr.at[0 : NZ - 3], ER)
        ef[0 : NZ * PAD, :] = ezr[...].astype(jnp.float32).reshape(NZ * PAD, LANES)

        for j in range(NCH):
            lanes = slice(j * LANES, (j + 1) * LANES)
            block[:, lanes] = ef[pl.ds(place(j), NZ, stride=PAD), :].astype(jnp.bfloat16)

        def features(x_of):
            return pl.ds(pl.multiple_of(first_chunk(x_of) * LANES, LANES), KW)

        for k in range(1, NX):
            to = lax.rem(x + k, NX)
            send(block.at[:, features(to)], part.at[x], KS, KR, at(to, z, pipe))

        for q, lanes in SHARES.items():

            @pl.when(pipe == q)
            def _(lanes=lanes):
                for k in range(1, NX):
                    to = at(lax.rem(x + k, NX), z, 1)
                    send(block.at[:, lanes], full.at[x, :, lanes], FS, FR, to)

        @pl.when(lead)
        def _():
            full[x] = block[...]

        part[x] = block[:, features(x)]
        wait_for(part.at[0:3], KR)
        scaled = part[...].reshape(NX * NZ, KW).astype(jnp.float32) * gl[:, features(x)]
        product = jnp.dot(
            scaled.astype(jnp.bfloat16), wk[...], preferred_element_type=jnp.float32
        )
        slot = y * NX + x
        kp[slot] = product.astype(jnp.bfloat16)
        for k in (2, 1, 3, 0):
            to = lax.rem(x + k, NX)

            def share(to=to):
                send(kp.at[slot], kp.at[slot], PS, PR, at(to, z, 1))

            if k:
                share()
            else:
                pl.when(jnp.logical_not(lead))(share)

    @pl.when(lead)
    def _():
        wait_for(full.at[0:3], FR)
        out = pltpu.make_async_copy(full, table_out, sem.at[O2])
        out.start()
        squares = jnp.zeros((NX * NZ, LANES), jnp.float32)
        for j in range(NCH):
            wide = full[:, :, LANES * j : LANES * (j + 1)].astype(jnp.float32)
            wide = wide.reshape(NX * NZ, LANES)
            squares = squares + wide * wide
        scale = lax.rsqrt(jnp.sum(squares, axis=-1, keepdims=True) / D + 1e-06)
        wait_for(kp.at[0 : NX * NP // 2 - 1], PR)
        for s in range(NP // 2):
            raw = kp[s * NX].astype(jnp.float32)
            for k in range(1, NX):
                raw = raw + kp[s * NX + k].astype(jnp.float32)
            raw = raw * scale
            for h in range(2):
                head = raw[:, h * HEAD_DIM : (h + 1) * HEAD_DIM]
                mean = jnp.mean(head * head, axis=-1, keepdims=True)
                first = s * HEADS2 + h * HEAD_DIM
                keys[:, first : first + HEAD_DIM] = (
                    head * lax.rsqrt(mean + 1e-06) * kg[...]
                ).astype(jnp.bfloat16)
        last_out = pltpu.make_async_copy(keys, keys_out, sem.at[O3])
        last_out.start()
        out.wait()
        last_out.wait()

    keep.wait()

    @pl.when(pipe == 0)
    def _():
        wait_for(gx, XS)

    @pl.when(last)
    def _():
        wait_for(gx.at[0 : NX - 1], XS)

    @pl.when(reducer)
    def _():
        wait_for(ezr.at[0 : NZ - 1], ZS)
        for q in range(NP - 1):
            wait_for(yr.at[0], YS)

    @pl.when(jnp.logical_not(worker))
    def _():
        wait_for(hz, WAS)
        wait_for(hz.at[0 : NZ - 1], WAS)

    @pl.when(worker)
    def _():
        wait_for(wc, W0S)
        wait_for(ezr.at[0 : NZ - 1], ES)
        wait_for(part.at[0:3], KS)
        wait_for(kp.at[0:3], PS)

        for q, lanes in SHARES.items():

            @pl.when(pipe == q)
            def _(lanes=lanes):
                wait_for(full.at[0 : NX - 1, :, lanes], FS)

        @pl.when(jnp.logical_not(lead))
        def _():
            wait_for(kp.at[0], PS)


PARTS, TOKENS_AT_ONCE = 3, 64


def look_up_kernel(
    table, keys, step, tokens,
    master_out, one_out, two_out, section_input, section_keys,
    table_v, keys_v, step_v, tokens_v, rows_v, looked, looked_keys, sem,
):
    lead = lax.axis_index("pipe") == 1
    width = D // PARTS

    def move(src, dst, which):
        copy = pltpu.make_async_copy(src, dst, sem.at[which])
        copy.start()
        return copy

    def give(first):
        rows = slice(first, first + TOKENS_AT_ONCE)
        return move(looked.at[rows], section_input.at[rows], first // TOKENS_AT_ONCE)

    load_step = move(step, step_v, 6)

    def finish(gives):
        load_step.wait()
        for j in range(NCH):
            lanes = slice(j * LANES, (j + 1) * LANES)
            for k in range(3):
                rows_v[k, :, lanes] = step_v[k, place(j) : place(j) + 1, :]
        for k, out in enumerate((master_out, one_out, two_out)):
            gives.append(move(rows_v.at[k], out, 11 + k))
        for copy in gives:
            copy.wait()

    @pl.when(lead)
    def _():
        load_tokens = move(tokens, tokens_v, 7)
        loads = []
        for part in range(PARTS):
            lanes = slice(part * width, (part + 1) * width)
            loads.append(move(table.at[:, :, lanes], table_v.at[:, :, lanes], 14 + part))
        load_keys = move(keys, keys_v, 9)
        load_tokens.wait()
        rows = lax.broadcasted_iota(jnp.int32, (NX * NZ, tokens_v.shape[1]), 0)
        hot = jnp.where(rows == tokens_v[...], 1.0, 0.0).T.astype(jnp.bfloat16)
        gives = []
        for copy in loads:
            copy.wait()
        for first in range(0, looked.shape[0], TOKENS_AT_ONCE):
            tokens_now = slice(first, first + TOKENS_AT_ONCE)
            for part in range(PARTS):
                lanes = slice(part * width, (part + 1) * width)
                looked[tokens_now, lanes] = jnp.dot(
                    hot[tokens_now], table_v[:, :, lanes].reshape(NX * NZ, width),
                    preferred_element_type=jnp.float32,
                ).astype(jnp.bfloat16)
            gives.append(give(first))
        load_keys.wait()
        looked_keys[...] = jnp.dot(
            hot, keys_v[...], preferred_element_type=jnp.float32
        ).astype(jnp.bfloat16)
        gives.append(move(looked_keys, section_keys, 10))
        finish(gives)

    @pl.when(jnp.logical_not(lead))
    def _():
        looked[...] = jnp.zeros_like(looked)
        looked_keys[...] = jnp.zeros_like(looked_keys)
        gives = [give(first) for first in range(0, looked.shape[0], TOKENS_AT_ONCE)]
        gives.append(move(looked_keys, section_keys, 10))
        finish(gives)


def shards(
    grad_partials, master, moment_one, moment_two, token_rows, input_gain, key_weight, key_gain
):
    rows, kvw, count = NX * NZ, NP * HEAD_DIM, token_rows.shape[0]
    bf16, f32 = jnp.bfloat16, jnp.float32
    hbm = pl.BlockSpec(memory_space=pl.ANY)
    table, keys, step = pl.pallas_call(
        comm_kernel,
        out_shape=(
            jax.ShapeDtypeStruct((NX, NZ, D), bf16),
            jax.ShapeDtypeStruct((rows, kvw), bf16),
            jax.ShapeDtypeStruct((3, PAD, LANES), f32),
        ),
        in_specs=[hbm] * 7,
        out_specs=(hbm,) * 3,
        scratch_shapes=[
            pltpu.VMEM((NX, NZ, D), bf16),
            pltpu.VMEM(((NZ + 1) * PAD, LANES), f32),
            pltpu.VMEM((NZ, PAD, LANES), bf16),
            pltpu.VMEM((2 * REACH, PAD, LANES), bf16),
            pltpu.VMEM((REACH, PAD, LANES), bf16),
            pltpu.VMEM((REACH - 1, PAD, LANES), bf16),
            pltpu.VMEM((2, PAD, LANES), bf16),
            pltpu.VMEM((2, PAD, LANES), f32),
            pltpu.VMEM((3, 1, D), f32),
            pltpu.VMEM((3, PAD, LANES), f32),
            pltpu.VMEM((PAD, LANES), bf16),
            pltpu.VMEM((NZ, PAD, LANES), bf16),
            pltpu.VMEM(((NZ + 1) * PAD, LANES), f32),
            pltpu.VMEM((NZ, D), bf16),
            pltpu.VMEM((NX, NZ, D), bf16),
            pltpu.VMEM((NX, NZ, KW), bf16),
            pltpu.VMEM((WROWS, LANES), bf16),
            pltpu.VMEM((WPAD, LANES), bf16),
            pltpu.VMEM((WPAD, HEADS2), bf16),
            pltpu.VMEM((NZ, WPAD, HEADS2), bf16),
            pltpu.VMEM((4, 4, WPAD, HEADS2), bf16),
            pltpu.VMEM((WPAD, LANES), f32),
            pltpu.VMEM((KW, HEADS2), bf16),
            pltpu.VMEM((NX * NP // 2, rows, HEADS2), bf16),
            pltpu.VMEM((NCH, LANES), f32),
            pltpu.VMEM((1, D), f32),
            pltpu.VMEM((1, HEAD_DIM), f32),
            pltpu.VMEM((3, PAD, LANES), f32),
            pltpu.VMEM((rows, kvw), bf16),
            pltpu.SemaphoreType.DMA((SEMS,)),
        ],
        compiler_params=pltpu.CompilerParams(
            collective_id=0, has_side_effects=True, vmem_limit_bytes=VMEM_BYTES
        ),
        name="sum_step_gather",
    )(
        grad_partials, master, moment_one, moment_two, key_weight,
        input_gain.reshape(NCH, LANES), key_gain.reshape(1, HEAD_DIM),
    )
    line = jax.ShapeDtypeStruct((1, D), f32)
    new_master, new_one, new_two, section_input, section_keys = pl.pallas_call(
        look_up_kernel,
        out_shape=(
            line, line, line,
            jax.ShapeDtypeStruct((count, D), bf16),
            jax.ShapeDtypeStruct((count, kvw), bf16),
        ),
        in_specs=[hbm] * 4,
        out_specs=(hbm,) * 5,
        scratch_shapes=[
            pltpu.VMEM((NX, NZ, D), bf16),
            pltpu.VMEM((rows, kvw), bf16),
            pltpu.VMEM((3, PAD, LANES), f32),
            pltpu.VMEM((1, count), jnp.int32),
            pltpu.VMEM((3, 1, D), f32),
            pltpu.VMEM((count, D), bf16),
            pltpu.VMEM((count, kvw), bf16),
            pltpu.SemaphoreType.DMA((14 + PARTS,)),
        ],
        compiler_params=pltpu.CompilerParams(vmem_limit_bytes=VMEM_BYTES),
        name="look_up",
    )(table, keys, step, token_rows.reshape(1, count))
    return new_master, new_one, new_two, section_input[None], section_keys[None]


def solution(mesh):
    in_specs = (
        P("pipe", "dp", None, None),
        P("dp", None),
        P("dp", None),
        P("dp", None),
        P("dp"),
        P(),
        P("dp", "pipe"),
        P(),
    )
    out_specs = (
        P("dp", None),
        P("dp", None),
        P("dp", None),
        P("pipe", "dp", None),
        P("pipe", "dp", None),
    )
    return jax.shard_map(shards, mesh=mesh, in_specs=in_specs, out_specs=out_specs, check_vma=False)
```
